512 devices in a mesh: ctx: 128 (over y, z_hi, x, core), tp: 4 (over z_lo).
Axes of the slice: x: 4, y: 8, z: 8 (z_hi: 2, z_lo: 4; z = z_hi * 4 + z_lo), core: 2. Of those that a mesh axis runs over, the one named last changes fastest.
Arguments:
- saved_rows: bfloat16 [16384, 3, 8192], P(('ctx', 'tp')), may hold values from -1.5 to 1.5
- grad_out: bfloat16 [16384, 8192], P('ctx', 'tp'), may hold values from -6 to 6
- conv_out: bfloat16 [16384, 8192], P('ctx', 'tp'), may hold values from -6 to 6
- filters: float32 [16384, 512], P('ctx', 'tp'), may hold values from -0.1875 to 0.1875
Outputs:
- d_saved: bfloat16 [16384, 3, 8192], P(('ctx', 'tp'))
- d_filters: float32 [16384, 512], P('ctx', 'tp')
The draws below stay inside these ranges and needn't reach their ends.
All inputs are finite; a program needn't handle non-finite values.
Results may differ from the reference program's by a relative error of at most 0.0049.
Values may be sent and summed in bfloat16 or wider, within the bound.
No kernel may reach another device: no remote copies, remote signals or barrier semaphores. Data moves between devices by JAX's collectives and lax.ppermute only.
A program may use at most 128 MiB of HBM per device.

```python
import jax
import jax.numpy as jnp
from jax import lax

D = 8192
GSIZE = 16
GROUPS = 512
SEQ = 16384
NFFT = 32768


def level_of(rng, shape, split, smallest, high):
    def one(position, parts):
        heights = jax.random.uniform(jax.random.fold_in(jax.random.fold_in(rng, 6), position), (parts,), jnp.float32, smallest / len(split), high / len(split))
        return jnp.repeat(jnp.exp(heights), shape[position] // parts).reshape((-1,) + (1,) * (len(shape) - position - 1))

    factor_of = one(*split[0])
    for cut in split[1:]:
        factor_of = factor_of * one(*cut)
    return factor_of


def bell_draw(own_key, extent, deviation, reach, pieces=(), dtype=jnp.bfloat16):
    level = level_of(own_key, extent, pieces, -0.22, 0.18) if pieces else 1.0
    result = jax.random.normal(own_key, extent, jnp.float32) * deviation * level
    return jnp.minimum(jnp.maximum(result, -reach), reach).astype(dtype)


def setup_inputs(seed: int = 0) -> dict:
    keys = jax.random.split(jax.random.key(seed), 5)
    return {
        "saved_rows": bell_draw(keys[0], (SEQ, 3, D), 0.25, 1.5, ((0, 512),)),
        "grad_out": bell_draw(keys[1], (SEQ, D), 1.0, 6.0, ((0, 128), (1, 4))),
        "conv_out": bell_draw(keys[2], (SEQ, D), 1.0, 6.0, ((0, 128), (1, 4))),
        "filters": bell_draw(keys[3], (SEQ, GROUPS), (SEQ // 16) ** -0.5, 0.1875, ((0, 128), (1, 4)), jnp.float32),
    }


def reference(saved_rows, grad_out, conv_out, filters):
    query_rows = saved_rows[:, 0, :].astype(jnp.float32)
    key_rows = saved_rows[:, 1, :].astype(jnp.float32)
    value_rows = saved_rows[:, 2, :].astype(jnp.float32)
    mixed = (key_rows * value_rows).astype(jnp.bfloat16)
    delta = (query_rows * grad_out.astype(jnp.float32)).astype(jnp.bfloat16)
    mixed_groups = mixed.reshape(SEQ, GROUPS, GSIZE).transpose(1, 0, 2)
    delta_groups = delta.reshape(SEQ, GROUPS, GSIZE).transpose(1, 0, 2)
    filter_groups = filters.T

    def one_group(items):
        part_x, part_dz, part_h = items
        spec_x = jnp.fft.rfft(part_x.astype(jnp.float32), n=NFFT, axis=0)
        spec_z = jnp.fft.rfft(part_dz.astype(jnp.float32), n=NFFT, axis=0)
        spec_h = jnp.fft.rfft(part_h, n=NFFT)
        grad_x = jnp.fft.irfft(jnp.conj(spec_h)[:, None] * spec_z, n=NFFT, axis=0)[:SEQ]
        grad_h = jnp.fft.irfft(jnp.sum(jnp.conj(spec_x) * spec_z, axis=1), n=NFFT)[:SEQ]
        return grad_x.astype(jnp.bfloat16), grad_h.astype(jnp.float32)

    grad_x, grad_h = lax.map(one_group, (mixed_groups, delta_groups, filter_groups))
    grad_x = grad_x.transpose(1, 0, 2).reshape(SEQ, D).astype(jnp.float32)
    d_query = (grad_out.astype(jnp.float32) * conv_out.astype(jnp.float32)).astype(jnp.bfloat16)
    d_key = (grad_x * value_rows).astype(jnp.bfloat16)
    d_value = (grad_x * key_rows).astype(jnp.bfloat16)
    return jnp.stack([d_query, d_key, d_value], axis=1), grad_h.T
```

```python
import jax
import jax.numpy as jnp
from jax import lax
from jax.experimental import pallas as pl
from jax.experimental.pallas import tpu as pltpu
from jax.sharding import PartitionSpec as P

GSIZE = 16
B = 128
F32 = jnp.float32
BF = jnp.bfloat16


def fill_pairs(src, which, dst):
    for half in range(2):
        dst[pl.ds(0, 1024), pl.ds(B * half, B)] = src[:, half, which].reshape(1024, B)


def correlate_kernel(h_ref, x_ref, o_ref, d_ref, f_ref, w_ref):
    fill_pairs(x_ref, 0, d_ref)
    d_ref[pl.ds(1024, 256), :] = jnp.zeros((256, 256), BF)
    row = lax.broadcasted_iota(jnp.int32, (B, B), 0)
    col = lax.broadcasted_iota(jnp.int32, (B, B), 1)
    flip = jnp.where((row + col) % B == 0, 1.0, 0.0).astype(BF)
    f_ref[...] = jnp.dot(h_ref[...], flip, preferred_element_type=F32)
    lower = row >= col

    def build(e, before):
        line = jnp.broadcast_to(f_ref[pl.ds(e, 1), :], (B, B))
        turned = pltpu.roll(line, 0, 1, stride=1, stride_axis=0)
        block = jnp.where(lower, turned, before).astype(BF)
        at = pl.multiple_of(e * B, B)
        w_ref[pl.ds(at, B), pl.ds(0, B)] = block
        w_ref[pl.ds(at + B, B), pl.ds(B, B)] = block
        return turned

    w_ref[pl.ds(0, B), pl.ds(B, B)] = jnp.zeros((B, B), BF)
    lax.fori_loop(0, B, build, jnp.zeros((B, B), F32), unroll=2)
    for tile in range(4):
        def body(k, acc):
            at = pl.multiple_of(64 * k, 64)
            left = jnp.concatenate(
                [d_ref[pl.ds(256 * tile + at + 16 * u, 256), :] for u in range(4)], axis=1
            )
            right = w_ref[pl.ds(pl.multiple_of(1024 * k, 1024), 1024), :]
            return acc + jnp.dot(left, right, preferred_element_type=F32)

        acc = lax.fori_loop(0, 16 - 4 * tile, body, jnp.zeros((256, 256), F32))
        for half in range(2):
            part = acc[:, B * half : B * half + B].astype(BF)
            o_ref[pl.ds(16 * tile, 16), half] = part.reshape(16, 16, B)


def lags_kernel(x_ref, o_ref, d_ref, m_ref, t_ref, qa_ref, qb_ref):
    fill_pairs(x_ref, 0, d_ref)
    d_ref[pl.ds(1024, 256), :] = jnp.zeros((256, 256), BF)
    fill_pairs(x_ref, 1, m_ref)
    row = lax.broadcasted_iota(jnp.int32, (B, B), 0)
    col = lax.broadcasted_iota(jnp.int32, (B, B), 1)
    flip = jnp.where(row + col == B - 1, 1.0, 0.0).astype(BF)
    for half in range(2):
        t_ref[pl.ds(B * half, B), :] = lax.dot_general(
            flip,
            m_ref[:, pl.ds(B * half, B)],
            (((1,), (1,)), ((), ())),
            preferred_element_type=F32,
        ).astype(BF)
    for part in range(4):
        depth = 256 * (4 - part)

        def body(k, carry):
            e = 16 * part + k
            gram = jnp.dot(
                t_ref[:, pl.ds(0, depth)],
                d_ref[pl.ds(pl.multiple_of(16 * e, 16), depth), :],
                preferred_element_type=F32,
            )
            qa_ref[2 * e] = gram[:B, :B] + gram[B:, B:]
            qa_ref[2 * e + 1] = gram[:B, B:]
            qb_ref[e] = gram[B:, :B]
            return carry

        lax.fori_loop(0, 16, body, 0)
    qb_ref[64] = jnp.zeros((B, B), F32)
    qa_ref[128] = jnp.zeros((B, B), F32)
    keep = row + col >= B - 1

    def diagonals(e, carry):
        first = qa_ref[2 * e]
        second = qa_ref[2 * e + 1] + qb_ref[e + 1]
        third = qa_ref[2 * e + 2]
        for u, (here, ahead) in enumerate(((first, second), (second, third))):
            turned = pltpu.roll(jnp.where(keep, here, ahead), 1, 1, stride=1, stride_axis=0)
            o_ref[pl.ds(2 * e + u, 1), :] = jnp.sum(turned, axis=0, keepdims=True)
        return carry

    lax.fori_loop(0, 64, diagonals, 0)


def correlate(taps, signals):
    return pl.pallas_call(
        correlate_kernel,
        out_shape=jax.ShapeDtypeStruct((64, 2, GSIZE, B), BF),
        scratch_shapes=[
            pltpu.VMEM((1280, 256), BF),
            pltpu.VMEM((B, B), F32),
            pltpu.VMEM((129 * B, 256), BF),
        ],
        compiler_params=pltpu.CompilerParams(vmem_limit_bytes=32 << 20),
        cost_estimate=pl.CostEstimate(
            flops=160 * 2 * 256**3, bytes_accessed=3 << 20, transcendentals=0
        ),
    )(taps, signals)


def lags(signals):
    return pl.pallas_call(
        lags_kernel,
        out_shape=jax.ShapeDtypeStruct((B, B), F32),
        scratch_shapes=[
            pltpu.VMEM((1280, 256), BF),
            pltpu.VMEM((1024, 256), BF),
            pltpu.VMEM((256, 1024), BF),
            pltpu.VMEM((129, B, B), F32),
            pltpu.VMEM((65, B, B), F32),
        ],
        compiler_params=pltpu.CompilerParams(vmem_limit_bytes=32 << 20),
        cost_estimate=pl.CostEstimate(
            flops=160 * 2 * 256**3, bytes_accessed=3 << 20, transcendentals=0
        ),
    )(signals)


def swap(x, axis):
    return lax.all_to_all(x, axis, split_axis=0, concat_axis=0, tiled=True)


def per_device(saved_rows, grad_out, conv_out, filters):
    rows, _, width = saved_rows.shape
    tokens, own = grad_out.shape
    parts = width // own
    query, key, value = (saved_rows[:, i, :].astype(F32) for i in range(3))
    mixed_rows = (key * value).astype(BF)
    taps = swap(filters.T.astype(BF), "ctx")
    outward = jnp.stack(
        [x.reshape(rows, parts, own).transpose(1, 0, 2) for x in (saved_rows[:, 0, :], mixed_rows)],
        axis=1,
    )
    arrived = swap(outward, "tp")
    query_cols = arrived[:, 0].reshape(tokens, own).astype(F32)
    mixed = arrived[:, 1].reshape(tokens, own)
    grad_wide = grad_out.astype(F32)
    delta = (query_cols * grad_wide).astype(BF)
    blocks = own // GSIZE
    spread = jnp.stack(
        [delta.T.reshape(blocks, GSIZE, tokens), mixed.T.reshape(blocks, GSIZE, tokens)], axis=1
    )
    signals = swap(spread, "ctx").reshape(blocks // 2, 2, 2, GSIZE, tokens)
    grad_x = correlate(taps, signals).reshape(blocks, GSIZE, tokens)
    back_x = swap(grad_x, "ctx").reshape(own, tokens)
    d_query = (grad_wide * conv_out.astype(F32)).astype(BF)
    grad_h = lags(signals)
    back_h = swap(grad_h, "ctx")
    homeward = jnp.stack(
        [d_query.reshape(parts, rows, own), back_x.T.reshape(parts, rows, own)], axis=1
    )
    home = swap(homeward, "tp")
    d_query_rows, grad_rows = (
        home[:, i].transpose(1, 0, 2).reshape(rows, width) for i in range(2)
    )
    grad_rows = grad_rows.astype(F32)
    d_key = (grad_rows * value).astype(BF)
    d_value = (grad_rows * key).astype(BF)
    return (jnp.stack([d_query_rows, d_key, d_value], axis=1), back_h.T)


def solution(mesh):
    placed = (P(("ctx", "tp"), None, None), P("ctx", "tp"), P("ctx", "tp"), P("ctx", "tp"))
    return jax.shard_map(
        per_device,
        mesh=mesh,
        in_specs=placed,
        out_specs=(P(("ctx", "tp"), None, None), P("ctx", "tp")),
        check_vma=False,
    )
```

```python
import jax
import jax.numpy as jnp
from jax import lax
from jax.experimental import pallas as pl
from jax.experimental.pallas import tpu as pltpu
from jax.sharding import PartitionSpec as P

GSIZE = 16
B = 128
OUT_ROWS = 40
BACK_ROWS = 24
F32 = jnp.float32
BF = jnp.bfloat16


def pack_rows_kernel(s_ref, o_ref):
    o_ref[0, 0] = s_ref[0]
    o_ref[0, 1] = (s_ref[1].astype(F32) * s_ref[2].astype(F32)).astype(BF)


def pack_rows(saved, parts):
    _, rows, width = saved.shape
    own = width // parts
    return pl.pallas_call(
        pack_rows_kernel,
        grid=(parts,),
        in_specs=[pl.BlockSpec((3, rows, own), lambda t: (0, 0, t))],
        out_specs=pl.BlockSpec((1, 2, rows, own), lambda t: (t, 0, 0, 0)),
        out_shape=jax.ShapeDtypeStruct((parts, 2, rows, own), BF),
    )(saved)


def pack_groups_kernel(a_ref, g_ref, c_ref, h_ref, o_ref, q_ref):
    tokens, span = g_ref.shape
    count = span // GSIZE
    grad = g_ref[...].astype(F32)
    q_ref[...] = (grad * c_ref[...].astype(F32)).astype(BF)
    query = a_ref[:, 0].reshape(tokens, span).astype(F32)
    delta = (query * grad).astype(BF)
    o_ref[:, pl.ds(0, GSIZE), :] = delta.T.reshape(count, GSIZE, tokens)
    mixed = a_ref[:, 1].reshape(tokens, span)
    o_ref[:, pl.ds(GSIZE, GSIZE), :] = mixed.T.reshape(count, GSIZE, tokens)
    taps = h_ref[...].T
    o_ref[:, pl.ds(2 * GSIZE, 8), :] = jnp.broadcast_to(
        taps[:, None, :], (count, 8, tokens)
    ).astype(BF)


def pack_groups(arrived, grad_out, conv_out, filters):
    parts, _, rows, own = arrived.shape
    tokens = parts * rows
    groups = own // GSIZE
    return pl.pallas_call(
        pack_groups_kernel,
        in_specs=[pl.BlockSpec(memory_space=pltpu.VMEM)] * 4,
        out_specs=[pl.BlockSpec(memory_space=pltpu.VMEM)] * 2,
        out_shape=(
            jax.ShapeDtypeStruct((groups, OUT_ROWS, tokens), BF),
            jax.ShapeDtypeStruct((tokens, own), BF),
        ),
        compiler_params=pltpu.CompilerParams(vmem_limit_bytes=32 << 20),
    )(arrived, grad_out, conv_out, filters)


def correlate_kernel(x_ref, o_ref, d_ref, m_ref, t_ref, f_ref, w_ref, qa_ref, qb_ref, l_ref):
    for half in range(2):
        lanes = pl.ds(B * half, B)
        d_ref[pl.ds(0, 1024), lanes] = x_ref[:, half, :GSIZE].reshape(1024, B)
        m_ref[:, lanes] = x_ref[:, half, GSIZE : 2 * GSIZE].reshape(1024, B)
    d_ref[pl.ds(1024, 256), :] = jnp.zeros((256, 256), BF)
    row = lax.broadcasted_iota(jnp.int32, (B, B), 0)
    col = lax.broadcasted_iota(jnp.int32, (B, B), 1)

    flip = jnp.where((row + col) % B == 0, 1.0, 0.0).astype(BF)
    taps = x_ref[:, :, 2 * GSIZE :].astype(F32).reshape(1024, B).astype(BF)
    f_ref[...] = jnp.dot(taps, flip, preferred_element_type=F32).reshape(B, 8, B)
    lower = row >= col
    w_ref[pl.ds(0, B), pl.ds(B, B)] = jnp.zeros((B, B), BF)

    def build(e, before):
        line = jnp.broadcast_to(f_ref[pl.ds(e, 1)], (16, 8, B)).reshape(B, B)
        turned = pltpu.roll(line, 0, 1, stride=1, stride_axis=0)
        block = jnp.where(lower, turned, before).astype(BF)
        at = pl.multiple_of(e * B, B)
        w_ref[pl.ds(at, B), pl.ds(0, B)] = block
        w_ref[pl.ds(at + B, B), pl.ds(B, B)] = block
        return turned

    lax.fori_loop(0, B, build, jnp.zeros((B, B), F32), unroll=16)
    for tile in range(4):
        count = 64 - 16 * tile
        left = jnp.concatenate(
            [d_ref[pl.ds(256 * tile + 16 * u, 256), :] for u in range(count)], axis=1
        )
        total = jnp.dot(left, w_ref[pl.ds(0, 256 * count), :], preferred_element_type=F32)
        for half in range(2):
            part = total[:, B * half : B * half + B].astype(BF)
            o_ref[pl.ds(16 * tile, 16), half, pl.ds(0, GSIZE)] = part.reshape(16, GSIZE, B)

    mirror = jnp.where(row + col == B - 1, 1.0, 0.0).astype(BF)
    for half in range(2):
        t_ref[pl.ds(B * half, B), :] = lax.dot_general(
            mirror,
            m_ref[:, pl.ds(B * half, B)],
            (((1,), (1,)), ((), ())),
            preferred_element_type=F32,
        ).astype(BF)
    for part in range(4):
        depth = 256 * (4 - part)

        def gram(k, carry):
            e = 16 * part + k
            table = jnp.dot(
                t_ref[:, pl.ds(0, depth)],
                d_ref[pl.ds(pl.multiple_of(16 * e, 16), depth), :],
                preferred_element_type=F32,
            )
            qa_ref[2 * e] = table[:B, :B] + table[B:, B:]
            qa_ref[2 * e + 1] = table[:B, B:]
            qb_ref[e] = table[B:, :B]
            return carry

        lax.fori_loop(0, 16, gram, 0, unroll=16)
    qb_ref[64] = jnp.zeros((B, B), F32)
    qa_ref[128] = jnp.zeros((B, B), F32)
    keep = row + col >= B - 1

    def diagonals(e, carry):
        first = qa_ref[2 * e]
        second = qa_ref[2 * e + 1] + qb_ref[e + 1]
        third = qa_ref[2 * e + 2]
        for u, (here, ahead) in enumerate(((first, second), (second, third))):
            turned = pltpu.roll(jnp.where(keep, here, ahead), 1, 1, stride=1, stride_axis=0)
            l_ref[pl.ds(2 * e + u, 1), :] = jnp.sum(turned, axis=0, keepdims=True)
        return carry

    lax.fori_loop(0, 64, diagonals, 0, unroll=16)
    sums = l_ref[...]
    coarse = sums.astype(BF).astype(F32)
    fine = sums - coarse
    shape = (B, 8, B)
    pick = lax.broadcasted_iota(jnp.int32, shape, 1) == 0
    both = jnp.where(
        pick, jnp.broadcast_to(coarse[:, None], shape), jnp.broadcast_to(fine[:, None], shape)
    )
    o_ref[:, :, pl.ds(GSIZE, 8)] = both.astype(BF).reshape(64, 2, 8, B)


def correlate(signals):
    return pl.pallas_call(
        correlate_kernel,
        in_specs=[pl.BlockSpec(memory_space=pltpu.VMEM)],
        out_specs=pl.BlockSpec(memory_space=pltpu.VMEM),
        out_shape=jax.ShapeDtypeStruct((64, 2, BACK_ROWS, B), BF),
        scratch_shapes=[
            pltpu.VMEM((1280, 256), BF),
            pltpu.VMEM((1024, 256), BF),
            pltpu.VMEM((256, 1024), BF),
            pltpu.VMEM((B, 8, B), F32),
            pltpu.VMEM((129 * B, 256), BF),
            pltpu.VMEM((129, B, B), F32),
            pltpu.VMEM((65, B, B), F32),
            pltpu.VMEM((B, B), F32),
        ],
        compiler_params=pltpu.CompilerParams(vmem_limit_bytes=40 << 20),
        cost_estimate=pl.CostEstimate(
            flops=640 * 2 * 256**3, bytes_accessed=64 << 20, transcendentals=0
        ),
    )(signals)


def unpack_groups_kernel(b_ref, x_ref, h_ref):
    groups = b_ref.shape[0]
    tokens = b_ref.shape[2]
    x_ref[...] = b_ref[:, :GSIZE].reshape(groups * GSIZE, tokens).T
    tail = b_ref[:, GSIZE:].astype(F32)
    row = lax.broadcasted_iota(jnp.int32, tail.shape, 1)
    h_ref[...] = jnp.sum(jnp.where(row < 2, tail, 0.0), axis=1).T


def unpack_groups(back):
    groups, _, tokens = back.shape
    return pl.pallas_call(
        unpack_groups_kernel,
        in_specs=[pl.BlockSpec(memory_space=pltpu.VMEM)],
        out_specs=[pl.BlockSpec(memory_space=pltpu.VMEM)] * 2,
        out_shape=(
            jax.ShapeDtypeStruct((tokens, groups * GSIZE), BF),
            jax.ShapeDtypeStruct((tokens, groups), F32),
        ),
        compiler_params=pltpu.CompilerParams(vmem_limit_bytes=32 << 20),
    )(back)


def finish_kernel(s_ref, q_ref, x_ref, o_ref):
    o_ref[0] = q_ref[0]
    grad = x_ref[0].astype(F32)
    o_ref[1] = (grad * s_ref[2].astype(F32)).astype(BF)
    o_ref[2] = (grad * s_ref[1].astype(F32)).astype(BF)


def finish(saved, d_query, grad_x):
    _, rows, width = saved.shape
    parts, _, own = grad_x.shape
    wide = pl.BlockSpec((3, rows, own), lambda t: (0, 0, t))
    one = pl.BlockSpec((1, rows, own), lambda t: (t, 0, 0))
    return pl.pallas_call(
        finish_kernel,
        grid=(parts,),
        in_specs=[wide, one, one],
        out_specs=wide,
        out_shape=jax.ShapeDtypeStruct(saved.shape, BF),
    )(saved, d_query, grad_x)


def swap(x, axis):
    return lax.all_to_all(x, axis, split_axis=0, concat_axis=0, tiled=True)


def per_device(saved_rows, grad_out, conv_out, filters):
    saved = saved_rows.transpose(1, 0, 2)
    _, rows, width = saved.shape
    tokens, own = grad_out.shape
    parts = width // own
    arrived = swap(pack_rows(saved, parts), "tp")
    spread, d_query = pack_groups(arrived, grad_out, conv_out, filters)
    signals, d_query = lax.optimization_barrier((swap(spread, "ctx"), d_query))
    groups = own // GSIZE
    home_q = swap(d_query.reshape(parts, rows, own), "tp")
    answer = correlate(signals.reshape(groups // 2, 2, OUT_ROWS, tokens))
    back = swap(answer.reshape(groups, BACK_ROWS, tokens), "ctx")
    grad_x, d_filters = unpack_groups(back)
    home_x = swap(grad_x.reshape(parts, rows, own), "tp")
    d_saved = finish(saved, home_q, home_x)
    return (d_saved.transpose(1, 0, 2), d_filters)


def solution(mesh):
    placed = (P(("ctx", "tp"), None, None), P("ctx", "tp"), P("ctx", "tp"), P("ctx", "tp"))
    return jax.shard_map(
        per_device,
        mesh=mesh,
        in_specs=placed,
        out_specs=(P(("ctx", "tp"), None, None), P("ctx", "tp")),
        check_vma=False,
    )
```

```python
import jax
import jax.numpy as jnp
from jax import lax
from jax.experimental import pallas as pl
from jax.experimental.pallas import tpu as pltpu
from jax.sharding import PartitionSpec as P

GSIZE = 16
B = 128
OUT_ROWS = 40
BACK_ROWS = 24
F32 = jnp.float32
BF = jnp.bfloat16


def pack_rows_kernel(me_ref, s_ref, *o_refs):
    parts = len(o_refs)
    own = o_refs[0].shape[2]
    for k, o_ref in enumerate(o_refs):
        lanes = pl.ds(pl.multiple_of((me_ref[0] + k) % parts * own, own), own)
        o_ref[0] = s_ref[0, :, lanes]
        o_ref[1] = (s_ref[1, :, lanes].astype(F32) * s_ref[2, :, lanes].astype(F32)).astype(BF)


def pack_rows(me, saved, parts):
    _, rows, width = saved.shape
    shape = jax.ShapeDtypeStruct((2, rows, width // parts), BF)
    return pl.pallas_call(
        pack_rows_kernel,
        in_specs=[
            pl.BlockSpec(memory_space=pltpu.SMEM),
            pl.BlockSpec(memory_space=pltpu.VMEM),
        ],
        out_specs=[pl.BlockSpec(memory_space=pltpu.VMEM)] * parts,
        out_shape=[shape] * parts,
        compiler_params=pltpu.CompilerParams(vmem_limit_bytes=32 << 20),
    )(me, saved)


def pack_groups_kernel(me_ref, g_ref, c_ref, h_ref, *refs):
    *a_refs, o_ref, q_ref, s_ref = refs
    parts = len(a_refs)
    tokens, span = g_ref.shape
    rows = tokens // parts
    count = span // GSIZE
    grad = g_ref[...].astype(F32)
    q_ref[...] = (grad * c_ref[...].astype(F32)).astype(BF)
    for k, a_ref in enumerate(a_refs):
        at = pl.multiple_of((me_ref[0] + parts - k) % parts * rows, rows)
        s_ref[0, pl.ds(at, rows), :] = a_ref[0]
        s_ref[1, pl.ds(at, rows), :] = a_ref[1]
    delta = (s_ref[0].astype(F32) * grad).astype(BF)
    o_ref[:, pl.ds(0, GSIZE), :] = delta.T.reshape(count, GSIZE, tokens)
    o_ref[:, pl.ds(GSIZE, GSIZE), :] = s_ref[1].T.reshape(count, GSIZE, tokens)
    taps = h_ref[...].T
    o_ref[:, pl.ds(2 * GSIZE, 8), :] = jnp.broadcast_to(
        taps[:, None, :], (count, 8, tokens)
    ).astype(BF)


def pack_groups(me, arrived, grad_out, conv_out, filters):
    tokens, own = grad_out.shape
    vmem = pl.BlockSpec(memory_space=pltpu.VMEM)
    return pl.pallas_call(
        pack_groups_kernel,
        in_specs=[pl.BlockSpec(memory_space=pltpu.SMEM)] + [vmem] * (3 + len(arrived)),
        out_specs=[vmem] * 2,
        out_shape=(
            jax.ShapeDtypeStruct((own // GSIZE, OUT_ROWS, tokens), BF),
            jax.ShapeDtypeStruct((tokens, own), BF),
        ),
        scratch_shapes=[pltpu.VMEM((2, tokens, own), BF)],
        compiler_params=pltpu.CompilerParams(vmem_limit_bytes=32 << 20),
    )(me, grad_out, conv_out, filters, *arrived)


def correlate_kernel(x_ref, o_ref, d_ref, m_ref, t_ref, f_ref, w_ref, qa_ref, qb_ref, l_ref):
    for half in range(2):
        lanes = pl.ds(B * half, B)
        d_ref[pl.ds(0, 1024), lanes] = x_ref[:, half, :GSIZE].reshape(1024, B)
        m_ref[:, lanes] = x_ref[:, half, GSIZE : 2 * GSIZE].reshape(1024, B)
    d_ref[pl.ds(1024, 256), :] = jnp.zeros((256, 256), BF)
    row = lax.broadcasted_iota(jnp.int32, (B, B), 0)
    col = lax.broadcasted_iota(jnp.int32, (B, B), 1)

    flip = jnp.where((row + col) % B == 0, 1.0, 0.0).astype(BF)
    taps = x_ref[:, :, 2 * GSIZE :].astype(F32).reshape(1024, B).astype(BF)
    f_ref[...] = jnp.dot(taps, flip, preferred_element_type=F32).reshape(B, 8, B)
    lower = row >= col
    w_ref[pl.ds(0, B), pl.ds(B, B)] = jnp.zeros((B, B), BF)

    def build(e, before):
        line = jnp.broadcast_to(f_ref[pl.ds(e, 1)], (16, 8, B)).reshape(B, B)
        turned = pltpu.roll(line, 0, 1, stride=1, stride_axis=0)
        block = jnp.where(lower, turned, before).astype(BF)
        at = pl.multiple_of(e * B, B)
        w_ref[pl.ds(at, B), pl.ds(0, B)] = block
        w_ref[pl.ds(at + B, B), pl.ds(B, B)] = block
        return turned

    lax.fori_loop(0, B, build, jnp.zeros((B, B), F32), unroll=16)
    for tile in range(4):
        count = 64 - 16 * tile
        left = jnp.concatenate(
            [d_ref[pl.ds(256 * tile + 16 * u, 256), :] for u in range(count)], axis=1
        )
        total = jnp.dot(left, w_ref[pl.ds(0, 256 * count), :], preferred_element_type=F32)
        for half in range(2):
            part = total[:, B * half : B * half + B].astype(BF)
            o_ref[pl.ds(16 * tile, 16), half, pl.ds(0, GSIZE)] = part.reshape(16, GSIZE, B)

    mirror = jnp.where(row + col == B - 1, 1.0, 0.0).astype(BF)
    for half in range(2):
        t_ref[pl.ds(B * half, B), :] = lax.dot_general(
            mirror,
            m_ref[:, pl.ds(B * half, B)],
            (((1,), (1,)), ((), ())),
            preferred_element_type=F32,
        ).astype(BF)
    for part in range(4):
        depth = 256 * (4 - part)

        def gram(k, carry):
            e = 16 * part + k
            table = jnp.dot(
                t_ref[:, pl.ds(0, depth)],
                d_ref[pl.ds(pl.multiple_of(16 * e, 16), depth), :],
                preferred_element_type=F32,
            )
            qa_ref[2 * e] = table[:B, :B] + table[B:, B:]
            qa_ref[2 * e + 1] = table[:B, B:]
            qb_ref[e] = table[B:, :B]
            return carry

        lax.fori_loop(0, 16, gram, 0, unroll=16)
    qb_ref[64] = jnp.zeros((B, B), F32)
    qa_ref[128] = jnp.zeros((B, B), F32)
    keep = row + col >= B - 1

    def diagonals(e, carry):
        first = qa_ref[2 * e]
        second = qa_ref[2 * e + 1] + qb_ref[e + 1]
        third = qa_ref[2 * e + 2]
        for u, (here, ahead) in enumerate(((first, second), (second, third))):
            turned = pltpu.roll(jnp.where(keep, here, ahead), 1, 1, stride=1, stride_axis=0)
            l_ref[pl.ds(2 * e + u, 1), :] = jnp.sum(turned, axis=0, keepdims=True)
        return carry

    lax.fori_loop(0, 64, diagonals, 0, unroll=16)
    sums = l_ref[...]
    coarse = sums.astype(BF).astype(F32)
    fine = sums - coarse
    shape = (B, 8, B)
    pick = lax.broadcasted_iota(jnp.int32, shape, 1) == 0
    both = jnp.where(
        pick, jnp.broadcast_to(coarse[:, None], shape), jnp.broadcast_to(fine[:, None], shape)
    )
    o_ref[:, :, pl.ds(GSIZE, 8)] = both.astype(BF).reshape(64, 2, 8, B)


def correlate(signals):
    return pl.pallas_call(
        correlate_kernel,
        in_specs=[pl.BlockSpec(memory_space=pltpu.VMEM)],
        out_specs=pl.BlockSpec(memory_space=pltpu.VMEM),
        out_shape=jax.ShapeDtypeStruct((64, 2, BACK_ROWS, B), BF),
        scratch_shapes=[
            pltpu.VMEM((1280, 256), BF),
            pltpu.VMEM((1024, 256), BF),
            pltpu.VMEM((256, 1024), BF),
            pltpu.VMEM((B, 8, B), F32),
            pltpu.VMEM((129 * B, 256), BF),
            pltpu.VMEM((129, B, B), F32),
            pltpu.VMEM((65, B, B), F32),
            pltpu.VMEM((B, B), F32),
        ],
        compiler_params=pltpu.CompilerParams(vmem_limit_bytes=40 << 20),
        cost_estimate=pl.CostEstimate(
            flops=640 * 2 * 256**3, bytes_accessed=64 << 20, transcendentals=0
        ),
    )(signals)


def unpack_groups_kernel(me_ref, b_ref, *refs):
    *x_refs, h_ref, s_ref = refs
    parts = len(x_refs)
    groups = b_ref.shape[0]
    tokens = b_ref.shape[2]
    rows = tokens // parts
    s_ref[...] = b_ref[:, :GSIZE].reshape(groups * GSIZE, tokens).T
    for k, x_ref in enumerate(x_refs):
        at = pl.multiple_of((me_ref[0] + k) % parts * rows, rows)
        x_ref[...] = s_ref[pl.ds(at, rows), :]
    tail = b_ref[:, GSIZE:].astype(F32)
    row = lax.broadcasted_iota(jnp.int32, tail.shape, 1)
    h_ref[...] = jnp.sum(jnp.where(row < 2, tail, 0.0), axis=1).T


def unpack_groups(me, back, parts):
    groups, _, tokens = back.shape
    vmem = pl.BlockSpec(memory_space=pltpu.VMEM)
    chunk = jax.ShapeDtypeStruct((tokens // parts, groups * GSIZE), BF)
    return pl.pallas_call(
        unpack_groups_kernel,
        in_specs=[pl.BlockSpec(memory_space=pltpu.SMEM), vmem],
        out_specs=[vmem] * (parts + 1),
        out_shape=[chunk] * parts + [jax.ShapeDtypeStruct((tokens, groups), F32)],
        scratch_shapes=[pltpu.VMEM((tokens, groups * GSIZE), BF)],
        compiler_params=pltpu.CompilerParams(vmem_limit_bytes=32 << 20),
    )(me, back)


def finish_kernel(me_ref, s_ref, q_ref, *refs):
    *x_refs, o_ref = refs
    o_ref[0] = q_ref[0]
    for k, x_ref in enumerate(x_refs):

        @pl.when(pl.program_id(0) == k)
        def _():
            grad = x_ref[...].astype(F32)
            o_ref[1] = (grad * s_ref[2].astype(F32)).astype(BF)
            o_ref[2] = (grad * s_ref[1].astype(F32)).astype(BF)


def finish(me, saved, d_query, grad_x):
    _, rows, width = saved.shape
    parts = len(grad_x)
    own = width // parts

    def source(k, me_ref):
        return (me_ref[0] + parts - k) % parts

    wide = pl.BlockSpec((3, rows, own), lambda k, m: (0, 0, source(k, m)))
    one = pl.BlockSpec((1, rows, own), lambda k, m: (source(k, m), 0, 0))
    whole = pl.BlockSpec((rows, own), lambda k, m: (0, 0))
    return pl.pallas_call(
        finish_kernel,
        grid_spec=pltpu.PrefetchScalarGridSpec(
            num_scalar_prefetch=1,
            grid=(parts,),
            in_specs=[wide, one] + [whole] * parts,
            out_specs=wide,
        ),
        out_shape=jax.ShapeDtypeStruct(saved.shape, BF),
    )(me, saved, d_query, *grad_x)


def swap(x, axis):
    return lax.all_to_all(x, axis, split_axis=0, concat_axis=0, tiled=True)


def shift(chunks, axis):
    size = len(chunks)
    return [chunks[0]] + [
        lax.ppermute(chunks[k], axis, [(i, (i + k) % size) for i in range(size)])
        for k in range(1, size)
    ]


def per_device(saved_rows, grad_out, conv_out, filters):
    saved = saved_rows.transpose(1, 0, 2)
    _, rows, width = saved.shape
    tokens, own = grad_out.shape
    parts = width // own
    groups = own // GSIZE
    me = lax.axis_index("tp").reshape(1)
    arrived = shift(pack_rows(me, saved, parts), "tp")
    spread, d_query = pack_groups(me, arrived, grad_out, conv_out, filters)
    signals, d_query = lax.optimization_barrier((swap(spread, "ctx"), d_query))
    home_q = swap(d_query.reshape(parts, rows, own), "tp")
    answer = correlate(signals.reshape(groups // 2, 2, OUT_ROWS, tokens))
    answer, home_q = lax.optimization_barrier((answer, home_q))
    back = swap(answer.reshape(groups, BACK_ROWS, tokens), "ctx")
    *grad_x, d_filters = unpack_groups(me, back, parts)
    d_saved = finish(me, saved, home_q, shift(grad_x, "tp"))
    return (d_saved.transpose(1, 0, 2), d_filters)


def solution(mesh):
    placed = (P(("ctx", "tp"), None, None), P("ctx", "tp"), P("ctx", "tp"), P("ctx", "tp"))
    return jax.shard_map(
        per_device,
        mesh=mesh,
        in_specs=placed,
        out_specs=(P(("ctx", "tp"), None, None), P("ctx", "tp")),
        check_vma=False,
    )
```

```python
import jax
import jax.numpy as jnp
from jax import lax
from jax.experimental import pallas as pl
from jax.experimental.pallas import tpu as pltpu
from jax.sharding import PartitionSpec as P

GSIZE = 16
B = 128
OUT_ROWS = 40
BACK_ROWS = 8
F32 = jnp.float32
BF = jnp.bfloat16


def pack_rows_kernel(me_ref, s_ref, *o_refs):
    parts = len(o_refs)
    own = o_refs[0].shape[2]
    for k, o_ref in enumerate(o_refs):
        lanes = pl.ds(pl.multiple_of((me_ref[0] + k) % parts * own, own), own)
        o_ref[0] = s_ref[0, :, lanes]
        o_ref[1] = (s_ref[1, :, lanes].astype(F32) * s_ref[2, :, lanes].astype(F32)).astype(BF)


def pack_rows(me, saved, parts):
    _, rows, width = saved.shape
    shape = jax.ShapeDtypeStruct((2, rows, width // parts), BF)
    return pl.pallas_call(
        pack_rows_kernel,
        in_specs=[
            pl.BlockSpec(memory_space=pltpu.SMEM),
            pl.BlockSpec(memory_space=pltpu.VMEM),
        ],
        out_specs=[pl.BlockSpec(memory_space=pltpu.VMEM)] * parts,
        out_shape=[shape] * parts,
        compiler_params=pltpu.CompilerParams(vmem_limit_bytes=32 << 20),
    )(me, saved)


def pack_groups_kernel(me_ref, g_ref, c_ref, h_ref, *refs):
    *a_refs, o_ref, q_ref, s_ref = refs
    parts = len(a_refs)
    tokens, span = g_ref.shape
    rows = tokens // parts
    count = span // GSIZE
    grad = g_ref[...].astype(F32)
    q_ref[...] = (grad * c_ref[...].astype(F32)).astype(BF)
    for k, a_ref in enumerate(a_refs):
        at = pl.multiple_of((me_ref[0] + parts - k) % parts * rows, rows)
        s_ref[0, pl.ds(at, rows), :] = a_ref[0]
        s_ref[1, pl.ds(at, rows), :] = a_ref[1]
    delta = (s_ref[0].astype(F32) * grad).astype(BF)
    o_ref[:, pl.ds(0, GSIZE), :] = delta.T.reshape(count, GSIZE, tokens)
    o_ref[:, pl.ds(GSIZE, GSIZE), :] = s_ref[1].T.reshape(count, GSIZE, tokens)
    taps = h_ref[...].T
    o_ref[:, pl.ds(2 * GSIZE, 8), :] = jnp.broadcast_to(
        taps[:, None, :], (count, 8, tokens)
    ).astype(BF)


def pack_groups(me, arrived, grad_out, conv_out, filters):
    tokens, own = grad_out.shape
    vmem = pl.BlockSpec(memory_space=pltpu.VMEM)
    return pl.pallas_call(
        pack_groups_kernel,
        in_specs=[pl.BlockSpec(memory_space=pltpu.SMEM)] + [vmem] * (3 + len(arrived)),
        out_specs=[vmem] * 2,
        out_shape=(
            jax.ShapeDtypeStruct((own // GSIZE, OUT_ROWS, tokens), BF),
            jax.ShapeDtypeStruct((tokens, own), BF),
        ),
        scratch_shapes=[pltpu.VMEM((2, tokens, own), BF)],
        compiler_params=pltpu.CompilerParams(vmem_limit_bytes=32 << 20),
    )(me, grad_out, conv_out, filters, *arrived)


def regroup(part, sums, o_ref, tile, half):
    shape = (16, 8, B)
    row = lax.broadcasted_iota(jnp.int32, shape, 1)
    lane = lax.broadcasted_iota(jnp.int32, shape, 2) // 32
    low, high = part[:, :8], part[:, 8:]
    fours = [low, jnp.roll(low, 4, axis=1), high, jnp.roll(high, 4, axis=1)]
    turned = []
    for d in range(4):
        mix = fours[(3 + d) % 4]
        for t in range(3):
            mix = jnp.where(lane == t, fours[(t + d) % 4], mix)
        turned.append(mix if d == 0 else jnp.roll(mix, 32 * d, axis=2))
    coarse = sums.astype(BF).astype(F32)
    fine = sums - coarse
    coarse = jnp.broadcast_to(coarse[:, None], shape)
    fine = jnp.broadcast_to(fine[:, None], shape)
    rest = jnp.where(row == 4, coarse, jnp.where(row == 5, fine, 0.0))
    for t in range(4):
        chunk = turned[(3 - t) % 4]
        for i in range(3):
            chunk = jnp.where(lane == i, turned[(i - t) % 4], chunk)
        o_ref[pl.ds(16 * tile, 16), half, t] = jnp.where(row < 4, chunk, rest).astype(BF)


def correlate_kernel(x_ref, o_ref, d_ref, m_ref, t_ref, f_ref, w_ref, qa_ref, qb_ref, l_ref):
    for half in range(2):
        lanes = pl.ds(B * half, B)
        d_ref[pl.ds(0, 1024), lanes] = x_ref[:, half, :GSIZE].reshape(1024, B)
        m_ref[:, lanes] = x_ref[:, half, GSIZE : 2 * GSIZE].reshape(1024, B)
    d_ref[pl.ds(1024, 256), :] = jnp.zeros((256, 256), BF)
    row = lax.broadcasted_iota(jnp.int32, (B, B), 0)
    col = lax.broadcasted_iota(jnp.int32, (B, B), 1)

    mirror = jnp.where(row + col == B - 1, 1.0, 0.0).astype(BF)
    for half in range(2):
        t_ref[pl.ds(B * half, B), :] = lax.dot_general(
            mirror,
            m_ref[:, pl.ds(B * half, B)],
            (((1,), (1,)), ((), ())),
            preferred_element_type=F32,
        ).astype(BF)
    for part in range(4):
        depth = 256 * (4 - part)

        def gram(k, carry):
            e = 16 * part + k
            table = jnp.dot(
                t_ref[:, pl.ds(0, depth)],
                d_ref[pl.ds(pl.multiple_of(16 * e, 16), depth), :],
                preferred_element_type=F32,
            )
            qa_ref[2 * e] = table[:B, :B] + table[B:, B:]
            qa_ref[2 * e + 1] = table[:B, B:]
            qb_ref[e] = table[B:, :B]
            return carry

        lax.fori_loop(0, 16, gram, 0, unroll=16)
    qb_ref[64] = jnp.zeros((B, B), F32)
    qa_ref[128] = jnp.zeros((B, B), F32)
    keep = row + col >= B - 1

    def diagonals(e, carry):
        first = qa_ref[2 * e]
        second = qa_ref[2 * e + 1] + qb_ref[e + 1]
        third = qa_ref[2 * e + 2]
        for u, (here, ahead) in enumerate(((first, second), (second, third))):
            turned = pltpu.roll(jnp.where(keep, here, ahead), 1, 1, stride=1, stride_axis=0)
            l_ref[pl.ds(2 * e + u, 1), :] = jnp.sum(turned, axis=0, keepdims=True)
        return carry

    lax.fori_loop(0, 64, diagonals, 0, unroll=16)
    flip = jnp.where((row + col) % B == 0, 1.0, 0.0).astype(BF)
    taps = x_ref[:, :, 2 * GSIZE :].astype(F32).reshape(1024, B).astype(BF)
    f_ref[...] = jnp.dot(taps, flip, preferred_element_type=F32).reshape(B, 8, B)
    lower = row >= col
    w_ref[pl.ds(0, B), pl.ds(B, B)] = jnp.zeros((B, B), BF)

    def build(e, before):
        line = jnp.broadcast_to(f_ref[pl.ds(e, 1)], (16, 8, B)).reshape(B, B)
        turned = pltpu.roll(line, 0, 1, stride=1, stride_axis=0)
        block = jnp.where(lower, turned, before).astype(BF)
        at = pl.multiple_of(e * B, B)
        w_ref[pl.ds(at, B), pl.ds(0, B)] = block
        w_ref[pl.ds(at + B, B), pl.ds(B, B)] = block
        return turned

    lax.fori_loop(0, B, build, jnp.zeros((B, B), F32), unroll=16)
    for tile in range(4):
        count = 64 - 16 * tile
        left = jnp.concatenate(
            [d_ref[pl.ds(256 * tile + 16 * u, 256), :] for u in range(count)], axis=1
        )
        total = jnp.dot(left, w_ref[pl.ds(0, 256 * count), :], preferred_element_type=F32)
        for half in range(2):
            part = total[:, B * half : B * half + B].reshape(16, GSIZE, B)
            sums = l_ref[pl.ds(32 * tile + half, 16, stride=2), :]
            regroup(part, sums, o_ref, tile, half)


def correlate(signals):
    return pl.pallas_call(
        correlate_kernel,
        in_specs=[pl.BlockSpec(memory_space=pltpu.VMEM)],
        out_specs=pl.BlockSpec(memory_space=pltpu.VMEM),
        out_shape=jax.ShapeDtypeStruct((64, 2, 4, BACK_ROWS, B), BF),
        scratch_shapes=[
            pltpu.VMEM((1280, 256), BF),
            pltpu.VMEM((1024, 256), BF),
            pltpu.VMEM((256, 1024), BF),
            pltpu.VMEM((B, 8, B), F32),
            pltpu.VMEM((129 * B, 256), BF),
            pltpu.VMEM((129, B, B), F32),
            pltpu.VMEM((65, B, B), F32),
            pltpu.VMEM((B, B), F32),
        ],
        compiler_params=pltpu.CompilerParams(vmem_limit_bytes=40 << 20),
        cost_estimate=pl.CostEstimate(
            flops=640 * 2 * 256**3, bytes_accessed=64 << 20, transcendentals=0
        ),
    )(signals)


def finish_kernel(me_ref, s_ref, q_ref, b_ref, o_ref, h_ref, l_ref, d_ref, sem):
    parts, rows, own = q_ref.shape
    steps = own // 256

    def send(source, plane, t):
        lanes = pl.ds(own * t, own)
        return pltpu.make_async_copy(source, o_ref.at[plane, :, lanes], sem.at[plane, t])

    copies = [send(q_ref.at[t], 0, t) for t in range(parts)]
    for copy in copies:
        copy.start()
    shape = (4 * B, 256)
    row = lax.broadcasted_iota(jnp.int32, shape, 0)
    col = lax.broadcasted_iota(jnp.int32, shape, 1)
    inner = row % B
    wanted = (inner // 8) * GSIZE + 4 * (row // B) + inner % 8
    spread = jnp.where((inner % 8 < 4) & (col == wanted), 1.0, 0.0).astype(BF)
    for t in range(parts):
        chunk = b_ref[:, t].astype(F32).reshape(B * 8, B).astype(BF).T
        for i in range(4):
            for b in range(steps):
                l_ref[pl.ds((t * steps + b) * rows, rows), pl.ds(B * i, B)] = chunk[
                    rows * i : rows * i + rows, B * b : B * b + B
                ]
        span = steps * rows
        grad = jnp.dot(
            l_ref[pl.ds(t * span, span), :], spread, preferred_element_type=F32
        )
        for b in range(steps):
            lanes = pl.ds(own * t + 256 * b, 256)
            here = grad[b * rows : b * rows + rows]
            d_ref[0, :, lanes] = (here * s_ref[2, :, lanes].astype(F32)).astype(BF)
            d_ref[1, :, lanes] = (here * s_ref[1, :, lanes].astype(F32)).astype(BF)
        for plane in (1, 2):
            copy = send(d_ref.at[plane - 1, :, pl.ds(own * t, own)], plane, t)
            copy.start()
            copies.append(copy)
    tail = b_ref[:, pl.ds(me_ref[0], 1)].reshape(b_ref.shape[0], 8, B).astype(F32)
    line = lax.broadcasted_iota(jnp.int32, tail.shape, 1)
    h_ref[...] = jnp.sum(jnp.where((line == 4) | (line == 5), tail, 0.0), axis=1).T
    for copy in copies:
        copy.wait()


def finish(me, saved, d_query, back):
    _, rows, width = saved.shape
    parts, _, own = d_query.shape
    vmem = pl.BlockSpec(memory_space=pltpu.VMEM)
    return pl.pallas_call(
        finish_kernel,
        in_specs=[pl.BlockSpec(memory_space=pltpu.SMEM), vmem, vmem, vmem],
        out_specs=[pl.BlockSpec(memory_space=pl.ANY), vmem],
        out_shape=(
            jax.ShapeDtypeStruct(saved.shape, BF),
            jax.ShapeDtypeStruct((B, own // GSIZE), F32),
        ),
        scratch_shapes=[
            pltpu.VMEM((parts * (own // 256) * rows, 4 * B), BF),
            pltpu.VMEM((2, rows, width), BF),
            pltpu.SemaphoreType.DMA((3, parts)),
        ],
        compiler_params=pltpu.CompilerParams(vmem_limit_bytes=32 << 20),
    )(me, saved, d_query, back)


def swap(x, axis):
    return lax.all_to_all(x, axis, split_axis=0, concat_axis=0, tiled=True)


def shift(chunks, axis):
    size = len(chunks)
    return [chunks[0]] + [
        lax.ppermute(chunks[k], axis, [(i, (i + k) % size) for i in range(size)])
        for k in range(1, size)
    ]


def per_device(saved_rows, grad_out, conv_out, filters):
    saved = saved_rows.transpose(1, 0, 2)
    _, rows, width = saved.shape
    tokens, own = grad_out.shape
    parts = width // own
    groups = own // GSIZE
    me = lax.axis_index("tp").reshape(1)
    arrived = shift(pack_rows(me, saved, parts), "tp")
    spread, d_query = pack_groups(me, arrived, grad_out, conv_out, filters)
    signals, d_query = lax.optimization_barrier((swap(spread, "ctx"), d_query))
    home_q = swap(d_query.reshape(parts, rows, own), "tp")
    answer = correlate(signals.reshape(groups // 2, 2, OUT_ROWS, tokens))
    answer, home_q = lax.optimization_barrier((answer, home_q))
    back = swap(answer.reshape(groups * parts, BACK_ROWS, tokens), ("ctx", "tp"))
    back = back.reshape(groups, parts, BACK_ROWS, tokens)
    d_saved, d_filters = finish(me, saved, home_q, back)
    return (d_saved.transpose(1, 0, 2), d_filters)


def solution(mesh):
    placed = (P(("ctx", "tp"), None, None), P("ctx", "tp"), P("ctx", "tp"), P("ctx", "tp"))
    return jax.shard_map(
        per_device,
        mesh=mesh,
        in_specs=placed,
        out_specs=(P(("ctx", "tp"), None, None), P("ctx", "tp")),
        check_vma=False,
    )
```

```python
import jax
import jax.numpy as jnp
from jax import lax
from jax.experimental import pallas as pl
from jax.experimental.pallas import tpu as pltpu
from jax.sharding import PartitionSpec as P

GSIZE = 16
B = 128
OUT_ROWS = 40
BACK_ROWS = 6
F32 = jnp.float32
BF = jnp.bfloat16


def pack_rows_kernel(me_ref, s_ref, *o_refs):
    parts = len(o_refs)
    own = o_refs[0].shape[2]
    for k, o_ref in enumerate(o_refs):
        lanes = pl.ds(pl.multiple_of((me_ref[0] + k) % parts * own, own), own)
        o_ref[0] = s_ref[0, :, lanes]
        o_ref[1] = (s_ref[1, :, lanes].astype(F32) * s_ref[2, :, lanes].astype(F32)).astype(BF)


def pack_rows(me, saved, parts):
    _, rows, width = saved.shape
    shape = jax.ShapeDtypeStruct((2, rows, width // parts), BF)
    return pl.pallas_call(
        pack_rows_kernel,
        in_specs=[
            pl.BlockSpec(memory_space=pltpu.SMEM),
            pl.BlockSpec(memory_space=pltpu.VMEM),
        ],
        out_specs=[pl.BlockSpec(memory_space=pltpu.VMEM)] * parts,
        out_shape=[shape] * parts,
        compiler_params=pltpu.CompilerParams(vmem_limit_bytes=32 << 20),
    )(me, saved)


def pack_groups_kernel(me_ref, g_ref, c_ref, h_ref, *refs):
    *a_refs, o_ref, q_ref, s_ref = refs
    parts = len(a_refs)
    tokens, span = g_ref.shape
    rows = tokens // parts
    count = span // GSIZE
    grad = g_ref[...].astype(F32)
    q_ref[...] = (grad * c_ref[...].astype(F32)).astype(BF)
    for k, a_ref in enumerate(a_refs):
        at = pl.multiple_of((me_ref[0] + parts - k) % parts * rows, rows)
        s_ref[0, pl.ds(at, rows), :] = a_ref[0]
        s_ref[1, pl.ds(at, rows), :] = a_ref[1]
    delta = (s_ref[0].astype(F32) * grad).astype(BF)
    o_ref[:, pl.ds(0, GSIZE), :] = delta.T.reshape(count, GSIZE, tokens)
    o_ref[:, pl.ds(GSIZE, GSIZE), :] = s_ref[1].T.reshape(count, GSIZE, tokens)
    taps = h_ref[...].T
    o_ref[:, pl.ds(2 * GSIZE, 8), :] = jnp.broadcast_to(
        taps[:, None, :], (count, 8, tokens)
    ).astype(BF)


def pack_groups(me, arrived, grad_out, conv_out, filters):
    tokens, own = grad_out.shape
    vmem = pl.BlockSpec(memory_space=pltpu.VMEM)
    return pl.pallas_call(
        pack_groups_kernel,
        in_specs=[pl.BlockSpec(memory_space=pltpu.SMEM)] + [vmem] * (3 + len(arrived)),
        out_specs=[vmem] * 2,
        out_shape=(
            jax.ShapeDtypeStruct((own // GSIZE, OUT_ROWS, tokens), BF),
            jax.ShapeDtypeStruct((tokens, own), BF),
        ),
        scratch_shapes=[pltpu.VMEM((2, tokens, own), BF)],
        compiler_params=pltpu.CompilerParams(vmem_limit_bytes=32 << 20),
    )(me, grad_out, conv_out, filters, *arrived)


def regroup(part, sums, o_ref, tile, half):
    shape = (16, 8, B)
    row = lax.broadcasted_iota(jnp.int32, shape, 1)
    lane = lax.broadcasted_iota(jnp.int32, shape, 2) // 32
    low, high = part[:, :8], part[:, 8:]
    fours = [low, jnp.roll(low, 4, axis=1), high, jnp.roll(high, 4, axis=1)]
    turned = []
    for d in range(4):
        mix = fours[(3 + d) % 4]
        for t in range(3):
            mix = jnp.where(lane == t, fours[(t + d) % 4], mix)
        turned.append(mix if d == 0 else jnp.roll(mix, 32 * d, axis=2))
    coarse = sums.astype(BF).astype(F32)
    fine = sums - coarse
    coarse = jnp.broadcast_to(coarse[:, None], shape)
    fine = jnp.broadcast_to(fine[:, None], shape)
    rest = jnp.where(row == 4, coarse, jnp.where(row == 5, fine, 0.0))
    chunks = []
    for t in range(4):
        chunk = turned[(3 - t) % 4]
        for i in range(3):
            chunk = jnp.where(lane == i, turned[(i - t) % 4], chunk)
        chunk = jnp.where(row < 4, chunk, rest)
        chunks.append(chunk if t == 0 else jnp.roll(chunk, 8 - 2 * t, axis=1))
    for u in range(3):
        joined = jnp.where(row < 6 - 2 * u, chunks[u], chunks[u + 1])
        o_ref[pl.ds(16 * tile, 16), half, pl.ds(8 * u, 8)] = joined.astype(BF)


def correlate_kernel(x_ref, o_ref, d_ref, m_ref, t_ref, f_ref, w_ref, qa_ref, qb_ref, l_ref):
    for half in range(2):
        lanes = pl.ds(B * half, B)
        d_ref[pl.ds(0, 1024), lanes] = x_ref[:, half, :GSIZE].reshape(1024, B)
        m_ref[:, lanes] = x_ref[:, half, GSIZE : 2 * GSIZE].reshape(1024, B)
    d_ref[pl.ds(1024, 256), :] = jnp.zeros((256, 256), BF)
    row = lax.broadcasted_iota(jnp.int32, (B, B), 0)
    col = lax.broadcasted_iota(jnp.int32, (B, B), 1)

    mirror = jnp.where(row + col == B - 1, 1.0, 0.0).astype(BF)
    for half in range(2):
        t_ref[pl.ds(B * half, B), :] = lax.dot_general(
            mirror,
            m_ref[:, pl.ds(B * half, B)],
            (((1,), (1,)), ((), ())),
            preferred_element_type=F32,
        ).astype(BF)
    for part in range(4):
        depth = 256 * (4 - part)

        def gram(k, carry):
            e = 16 * part + k
            table = jnp.dot(
                t_ref[:, pl.ds(0, depth)],
                d_ref[pl.ds(pl.multiple_of(16 * e, 16), depth), :],
                preferred_element_type=F32,
            )
            qa_ref[2 * e] = table[:B, :B] + table[B:, B:]
            qa_ref[2 * e + 1] = table[:B, B:]
            qb_ref[e] = table[B:, :B]
            return carry

        lax.fori_loop(0, 16, gram, 0, unroll=16)
    qb_ref[64] = jnp.zeros((B, B), F32)
    qa_ref[128] = jnp.zeros((B, B), F32)
    keep = row + col >= B - 1

    def diagonals(e, carry):
        first = qa_ref[2 * e]
        second = qa_ref[2 * e + 1] + qb_ref[e + 1]
        third = qa_ref[2 * e + 2]
        for u, (here, ahead) in enumerate(((first, second), (second, third))):
            turned = pltpu.roll(jnp.where(keep, here, ahead), 1, 1, stride=1, stride_axis=0)
            l_ref[pl.ds(2 * e + u, 1), :] = jnp.sum(turned, axis=0, keepdims=True)
        return carry

    lax.fori_loop(0, 64, diagonals, 0, unroll=16)
    flip = jnp.where((row + col) % B == 0, 1.0, 0.0).astype(BF)
    taps = x_ref[:, :, 2 * GSIZE :].astype(F32).reshape(1024, B).astype(BF)
    f_ref[...] = jnp.dot(taps, flip, preferred_element_type=F32).reshape(B, 8, B)
    lower = row >= col
    w_ref[pl.ds(0, B), pl.ds(B, B)] = jnp.zeros((B, B), BF)

    def build(e, before):
        line = jnp.broadcast_to(f_ref[pl.ds(e, 1)], (16, 8, B)).reshape(B, B)
        turned = pltpu.roll(line, 0, 1, stride=1, stride_axis=0)
        block = jnp.where(lower, turned, before).astype(BF)
        at = pl.multiple_of(e * B, B)
        w_ref[pl.ds(at, B), pl.ds(0, B)] = block
        w_ref[pl.ds(at + B, B), pl.ds(B, B)] = block
        return turned

    lax.fori_loop(0, B, build, jnp.zeros((B, B), F32), unroll=16)
    for tile in range(4):
        count = 64 - 16 * tile
        left = jnp.concatenate(
            [d_ref[pl.ds(256 * tile + 16 * u, 256), :] for u in range(count)], axis=1
        )
        total = jnp.dot(left, w_ref[pl.ds(0, 256 * count), :], preferred_element_type=F32)
        for half in range(2):
            part = total[:, B * half : B * half + B].reshape(16, GSIZE, B)
            sums = l_ref[pl.ds(32 * tile + half, 16, stride=2), :]
            regroup(part, sums, o_ref, tile, half)


def correlate(signals):
    return pl.pallas_call(
        correlate_kernel,
        in_specs=[pl.BlockSpec(memory_space=pltpu.VMEM)],
        out_specs=pl.BlockSpec(memory_space=pltpu.VMEM),
        out_shape=jax.ShapeDtypeStruct((64, 2, 4 * BACK_ROWS, B), BF),
        scratch_shapes=[
            pltpu.VMEM((1280, 256), BF),
            pltpu.VMEM((1024, 256), BF),
            pltpu.VMEM((256, 1024), BF),
            pltpu.VMEM((B, 8, B), F32),
            pltpu.VMEM((129 * B, 256), BF),
            pltpu.VMEM((129, B, B), F32),
            pltpu.VMEM((65, B, B), F32),
            pltpu.VMEM((B, B), F32),
        ],
        compiler_params=pltpu.CompilerParams(vmem_limit_bytes=40 << 20),
        cost_estimate=pl.CostEstimate(
            flops=640 * 2 * 256**3, bytes_accessed=64 << 20, transcendentals=0
        ),
    )(signals)


def finish_kernel(me_ref, s_ref, q_ref, b_ref, o_ref, h_ref, l_ref, d_ref, sem):
    parts, rows, own = q_ref.shape
    steps = own // 256

    def send(source, plane, t):
        lanes = pl.ds(own * t, own)
        return pltpu.make_async_copy(source, o_ref.at[plane, :, lanes], sem.at[plane, t])

    copies = [send(q_ref.at[t], 0, t) for t in range(parts)]
    for copy in copies:
        copy.start()
    shape = (4 * B, 256)
    row = lax.broadcasted_iota(jnp.int32, shape, 0)
    col = lax.broadcasted_iota(jnp.int32, shape, 1)
    inner = row % B
    wanted = (inner // 8) * GSIZE + 4 * (row // B) + inner % 8
    spread = jnp.where((inner % 8 < 4) & (col == wanted), 1.0, 0.0).astype(BF)
    tiles = [b_ref[:, pl.ds(8 * u, 8)].astype(F32) for u in range(3)]
    line = lax.broadcasted_iota(jnp.int32, tiles[0].shape, 1)
    chunks = [tiles[0]]
    for t in range(1, parts):
        part = jnp.roll(tiles[t - 1], 2 * t, axis=1)
        if t < parts - 1:
            part = jnp.where(line < 2 * t, part, jnp.roll(tiles[t], 2 * t, axis=1))
        chunks.append(part)
    for t in range(parts):
        chunk = chunks[t].reshape(B * 8, B).astype(BF).T
        for i in range(4):
            for b in range(steps):
                l_ref[pl.ds((t * steps + b) * rows, rows), pl.ds(B * i, B)] = chunk[
                    rows * i : rows * i + rows, B * b : B * b + B
                ]
        span = steps * rows
        grad = jnp.dot(
            l_ref[pl.ds(t * span, span), :], spread, preferred_element_type=F32
        )
        for b in range(steps):
            lanes = pl.ds(own * t + 256 * b, 256)
            here = grad[b * rows : b * rows + rows]
            d_ref[0, :, lanes] = (here * s_ref[2, :, lanes].astype(F32)).astype(BF)
            d_ref[1, :, lanes] = (here * s_ref[1, :, lanes].astype(F32)).astype(BF)
        for plane in (1, 2):
            copy = send(d_ref.at[plane - 1, :, pl.ds(own * t, own)], plane, t)
            copy.start()
            copies.append(copy)
    tail = chunks[0]
    for t in range(1, parts):
        tail = jnp.where(me_ref[0] == t, chunks[t], tail)
    h_ref[...] = jnp.sum(jnp.where((line == 4) | (line == 5), tail, 0.0), axis=1).T
    for copy in copies:
        copy.wait()


def finish(me, saved, d_query, back):
    _, rows, width = saved.shape
    parts, _, own = d_query.shape
    vmem = pl.BlockSpec(memory_space=pltpu.VMEM)
    return pl.pallas_call(
        finish_kernel,
        in_specs=[pl.BlockSpec(memory_space=pltpu.SMEM), vmem, vmem, vmem],
        out_specs=[pl.BlockSpec(memory_space=pl.ANY), vmem],
        out_shape=(
            jax.ShapeDtypeStruct(saved.shape, BF),
            jax.ShapeDtypeStruct((B, own // GSIZE), F32),
        ),
        scratch_shapes=[
            pltpu.VMEM((parts * (own // 256) * rows, 4 * B), BF),
            pltpu.VMEM((2, rows, width), BF),
            pltpu.SemaphoreType.DMA((3, parts)),
        ],
        compiler_params=pltpu.CompilerParams(vmem_limit_bytes=32 << 20),
    )(me, saved, d_query, back)


def swap(x, axis):
    return lax.all_to_all(x, axis, split_axis=0, concat_axis=0, tiled=True)


def shift(chunks, axis):
    size = len(chunks)
    return [chunks[0]] + [
        lax.ppermute(chunks[k], axis, [(i, (i + k) % size) for i in range(size)])
        for k in range(1, size)
    ]


def per_device(saved_rows, grad_out, conv_out, filters):
    saved = saved_rows.transpose(1, 0, 2)
    _, rows, width = saved.shape
    tokens, own = grad_out.shape
    parts = width // own
    groups = own // GSIZE
    me = lax.axis_index("tp").reshape(1)
    arrived = shift(pack_rows(me, saved, parts), "tp")
    spread, d_query = pack_groups(me, arrived, grad_out, conv_out, filters)
    signals, d_query = lax.optimization_barrier((swap(spread, "ctx"), d_query))
    home_q = swap(d_query.reshape(parts, rows, own), "tp")
    answer = correlate(signals.reshape(groups // 2, 2, OUT_ROWS, tokens))
    answer, home_q = lax.optimization_barrier((answer, home_q))
    back = swap(answer.reshape(groups * parts, BACK_ROWS // 2, 2, tokens), ("ctx", "tp"))
    back = back.reshape(groups, parts * BACK_ROWS, tokens)
    d_saved, d_filters = finish(me, saved, home_q, back)
    return (d_saved.transpose(1, 0, 2), d_filters)


def solution(mesh):
    placed = (P(("ctx", "tp"), None, None), P("ctx", "tp"), P("ctx", "tp"), P("ctx", "tp"))
    return jax.shard_map(
        per_device,
        mesh=mesh,
        in_specs=placed,
        out_specs=(P(("ctx", "tp"), None, None), P("ctx", "tp")),
        check_vma=False,
    )
```

```python
import jax
import jax.numpy as jnp
from jax import lax
from jax.experimental import pallas as pl
from jax.experimental.pallas import tpu as pltpu
from jax.sharding import PartitionSpec as P

GSIZE = 16
B = 128
OUT_ROWS = 10
BACK_ROWS = 6
F32 = jnp.float32
BF = jnp.bfloat16


def split_kernel(me_ref, g_ref, c_ref, *refs):
    *g_refs, q_ref = refs
    parts = len(g_refs)
    rows = g_refs[0].shape[0]
    for k, o_ref in enumerate(g_refs):
        at = pl.multiple_of((me_ref[0] + k) % parts * rows, rows)
        o_ref[...] = g_ref[pl.ds(at, rows), :]
    q_ref[...] = (g_ref[...].astype(F32) * c_ref[...].astype(F32)).astype(BF)


def split(me, grad_out, conv_out, parts):
    tokens, own = grad_out.shape
    vmem = pl.BlockSpec(memory_space=pltpu.VMEM)
    chunk = jax.ShapeDtypeStruct((tokens // parts, own), BF)
    return pl.pallas_call(
        split_kernel,
        in_specs=[pl.BlockSpec(memory_space=pltpu.SMEM), vmem, vmem],
        out_specs=[vmem] * (parts + 1),
        out_shape=[chunk] * parts + [jax.ShapeDtypeStruct((tokens, own), BF)],
        compiler_params=pltpu.CompilerParams(vmem_limit_bytes=32 << 20),
    )(me, grad_out, conv_out)


def pack_kernel(me_ref, s_ref, h_ref, *refs):
    *g_refs, o_ref, f_ref, l_ref, c_ref = refs
    parts = len(g_refs)
    rows, own = g_refs[0].shape
    steps = own // 256
    span = steps * rows
    for k, g_ref in enumerate(g_refs):
        source = (me_ref[0] + parts - k) % parts
        f_ref[pl.ds(pl.multiple_of(source * rows, rows), rows), :] = g_ref[...]
    shape = (512, 512)
    row = lax.broadcasted_iota(jnp.int32, shape, 0)
    col = lax.broadcasted_iota(jnp.int32, shape, 1)
    wanted = (row % 16) // 4 * B + (row % 256) // 16 * 8 + row // 256 * 4 + row % 4
    gather = jnp.where(col == wanted, 1.0, 0.0).astype(BF)
    for t in range(parts):
        grad = f_ref[pl.ds(rows * t, rows), :].astype(F32)
        lanes = pl.ds(own * t, own)
        delta = (s_ref[0, :, lanes].astype(F32) * grad).astype(BF)
        mixed = (s_ref[1, :, lanes].astype(F32) * s_ref[2, :, lanes].astype(F32)).astype(BF)
        for b in range(steps):
            at = pl.ds(b * rows, rows)
            l_ref[at, pl.ds(0, 256)] = delta[:, 256 * b : 256 * b + 256]
            l_ref[at, pl.ds(256, 256)] = mixed[:, 256 * b : 256 * b + 256]
        spread = jnp.dot(l_ref[...], gather, preferred_element_type=F32)
        for b in range(steps):
            here = spread[b * rows : b * rows + rows]
            block = jnp.concatenate([here[:, B * i : B * i + B] for i in range(4)], axis=0)
            c_ref[t, pl.ds(16 * b, 16)] = block.T.reshape(16, 8, B)
    taps = h_ref[...].T
    shape = (16, 8, B)
    line = lax.broadcasted_iota(jnp.int32, shape, 1)
    for b in range(8):
        groups = pl.ds(16 * b, 16)
        filt = jnp.broadcast_to(taps[16 * b : 16 * b + 16][:, None], shape)
        chunks = [c_ref[0, groups]] + [
            jnp.roll(c_ref[t, groups], 2 * t, axis=1) for t in range(1, parts)
        ]
        for u in range(5):
            tile = filt
            if u < parts:
                tile = jnp.where(line >= 2 * u, chunks[u], tile)
            if u > 0:
                tile = jnp.where(line < 2 * u - 2, chunks[u - 1], tile)
            o_ref[groups, pl.ds(8 * u, 8)] = tile.astype(BF)


def pack(me, saved, filters, grads):
    parts = len(grads)
    rows, own = grads[0].shape
    vmem = pl.BlockSpec(memory_space=pltpu.VMEM)
    return pl.pallas_call(
        pack_kernel,
        in_specs=[pl.BlockSpec(memory_space=pltpu.SMEM)] + [vmem] * (2 + parts),
        out_specs=vmem,
        out_shape=jax.ShapeDtypeStruct((own // GSIZE, parts * OUT_ROWS, B), BF),
        scratch_shapes=[
            pltpu.VMEM((parts * rows, own), BF),
            pltpu.VMEM((own // 256 * rows, 512), BF),
            pltpu.VMEM((parts, B, 8, B), F32),
        ],
        compiler_params=pltpu.CompilerParams(vmem_limit_bytes=32 << 20),
    )(me, saved, filters, *grads)


def ungroup(me, x_ref, d_ref, m_ref, n_ref):
    shape = (16, 8, B)
    line = lax.broadcasted_iota(jnp.int32, shape, 1)
    lane = lax.broadcasted_iota(jnp.int32, shape, 2) // 32
    for half in range(2):
        lanes = pl.ds(B * half, B)
        for b in range(4):
            pairs = pl.ds(16 * b, 16)
            tiles = [x_ref[pairs, half, pl.ds(8 * u, 8)].astype(F32) for u in range(5)]
            chunks = [tiles[0]] + [
                jnp.roll(jnp.where(line < 2 * t, tiles[t + 1], tiles[t]), 8 - 2 * t, axis=1)
                for t in range(1, 4)
            ]
            taps = jnp.where((line == 6) | (line == 7), tiles[4], 0.0)
            for t in range(3):
                here = jnp.where((line == 2 * t) | (line == 2 * t + 1), tiles[t + 1], 0.0)
                taps = jnp.where(me == t, here, taps)
            taps = jnp.broadcast_to(0.5 * jnp.sum(taps, axis=1, keepdims=True), shape)
            n_ref[pairs, half] = taps
            turned = []
            for d in range(4):
                mix = chunks[(3 - d) % 4]
                for i in range(3):
                    mix = jnp.where(lane == i, chunks[(i - d) % 4], mix)
                turned.append(mix if d == 0 else jnp.roll(mix, B - 32 * d, axis=2))
            fours = []
            for i in range(4):
                mix = turned[(i - 3) % 4]
                for t in range(3):
                    mix = jnp.where(lane == t, turned[(i - t) % 4], mix)
                fours.append(mix)
            moved = [jnp.roll(x, 4, axis=1) for x in fours]
            top = line < 4
            delta = [jnp.where(top, fours[i], moved[i + 1]) for i in (0, 2)]
            mixed = [jnp.where(top, moved[i], fours[i + 1]) for i in (0, 2)]
            at = pl.ds(256 * b, 256)
            d_ref[at, lanes] = jnp.concatenate(delta, axis=1).reshape(256, B).astype(BF)
            m_ref[at, lanes] = jnp.concatenate(mixed, axis=1).reshape(256, B).astype(BF)


def regroup(part, sums, o_ref, tile, half):
    shape = (16, 8, B)
    row = lax.broadcasted_iota(jnp.int32, shape, 1)
    lane = lax.broadcasted_iota(jnp.int32, shape, 2) // 32
    low, high = part[:, :8], part[:, 8:]
    fours = [low, jnp.roll(low, 4, axis=1), high, jnp.roll(high, 4, axis=1)]
    turned = []
    for d in range(4):
        mix = fours[(3 + d) % 4]
        for t in range(3):
            mix = jnp.where(lane == t, fours[(t + d) % 4], mix)
        turned.append(mix if d == 0 else jnp.roll(mix, 32 * d, axis=2))
    coarse = sums.astype(BF).astype(F32)
    fine = sums - coarse
    coarse = jnp.broadcast_to(coarse[:, None], shape)
    fine = jnp.broadcast_to(fine[:, None], shape)
    rest = jnp.where(row == 4, coarse, jnp.where(row == 5, fine, 0.0))
    chunks = []
    for t in range(4):
        chunk = turned[(3 - t) % 4]
        for i in range(3):
            chunk = jnp.where(lane == i, turned[(i - t) % 4], chunk)
        chunk = jnp.where(row < 4, chunk, rest)
        chunks.append(chunk if t == 0 else jnp.roll(chunk, 8 - 2 * t, axis=1))
    for u in range(3):
        joined = jnp.where(row < 6 - 2 * u, chunks[u], chunks[u + 1])
        o_ref[pl.ds(16 * tile, 16), half, pl.ds(8 * u, 8)] = joined.astype(BF)


def correlate_kernel(
    me_ref, x_ref, o_ref, d_ref, m_ref, t_ref, f_ref, w_ref, qa_ref, qb_ref, l_ref, n_ref
):
    ungroup(me_ref[0], x_ref, d_ref, m_ref, n_ref)
    d_ref[pl.ds(1024, 256), :] = jnp.zeros((256, 256), BF)
    row = lax.broadcasted_iota(jnp.int32, (B, B), 0)
    col = lax.broadcasted_iota(jnp.int32, (B, B), 1)

    mirror = jnp.where(row + col == B - 1, 1.0, 0.0).astype(BF)
    for half in range(2):
        t_ref[pl.ds(B * half, B), :] = lax.dot_general(
            mirror,
            m_ref[:, pl.ds(B * half, B)],
            (((1,), (1,)), ((), ())),
            preferred_element_type=F32,
        ).astype(BF)
    for part in range(4):
        depth = 256 * (4 - part)

        def gram(k, carry):
            e = 16 * part + k
            table = jnp.dot(
                t_ref[:, pl.ds(0, depth)],
                d_ref[pl.ds(pl.multiple_of(16 * e, 16), depth), :],
                preferred_element_type=F32,
            )
            qa_ref[2 * e] = table[:B, :B] + table[B:, B:]
            qa_ref[2 * e + 1] = table[:B, B:]
            qb_ref[e] = table[B:, :B]
            return carry

        lax.fori_loop(0, 16, gram, 0, unroll=16)
    qb_ref[64] = jnp.zeros((B, B), F32)
    qa_ref[128] = jnp.zeros((B, B), F32)
    keep = row + col >= B - 1

    def diagonals(e, carry):
        first = qa_ref[2 * e]
        second = qa_ref[2 * e + 1] + qb_ref[e + 1]
        third = qa_ref[2 * e + 2]
        for u, (here, ahead) in enumerate(((first, second), (second, third))):
            turned = pltpu.roll(jnp.where(keep, here, ahead), 1, 1, stride=1, stride_axis=0)
            l_ref[pl.ds(2 * e + u, 1), :] = jnp.sum(turned, axis=0, keepdims=True)
        return carry

    lax.fori_loop(0, 64, diagonals, 0, unroll=16)
    flip = jnp.where((row + col) % B == 0, 1.0, 0.0).astype(BF)
    taps = n_ref[...].reshape(1024, B).astype(BF)
    f_ref[...] = jnp.dot(taps, flip, preferred_element_type=F32).reshape(B, 8, B)
    lower = row >= col
    w_ref[pl.ds(0, B), pl.ds(B, B)] = jnp.zeros((B, B), BF)

    def build(e, before):
        line = jnp.broadcast_to(f_ref[pl.ds(e, 1)], (16, 8, B)).reshape(B, B)
        turned = pltpu.roll(line, 0, 1, stride=1, stride_axis=0)
        block = jnp.where(lower, turned, before).astype(BF)
        at = pl.multiple_of(e * B, B)
        w_ref[pl.ds(at, B), pl.ds(0, B)] = block
        w_ref[pl.ds(at + B, B), pl.ds(B, B)] = block
        return turned

    lax.fori_loop(0, B, build, jnp.zeros((B, B), F32), unroll=16)
    for tile in range(4):
        count = 64 - 16 * tile
        left = jnp.concatenate(
            [d_ref[pl.ds(256 * tile + 16 * u, 256), :] for u in range(count)], axis=1
        )
        total = jnp.dot(left, w_ref[pl.ds(0, 256 * count), :], preferred_element_type=F32)
        for half in range(2):
            part = total[:, B * half : B * half + B].reshape(16, GSIZE, B)
            sums = l_ref[pl.ds(32 * tile + half, 16, stride=2), :]
            regroup(part, sums, o_ref, tile, half)


def correlate(me, signals):
    return pl.pallas_call(
        correlate_kernel,
        in_specs=[
            pl.BlockSpec(memory_space=pltpu.SMEM),
            pl.BlockSpec(memory_space=pltpu.VMEM),
        ],
        out_specs=pl.BlockSpec(memory_space=pltpu.VMEM),
        out_shape=jax.ShapeDtypeStruct((64, 2, 4 * BACK_ROWS, B), BF),
        scratch_shapes=[
            pltpu.VMEM((1280, 256), BF),
            pltpu.VMEM((1024, 256), BF),
            pltpu.VMEM((256, 1024), BF),
            pltpu.VMEM((B, 8, B), F32),
            pltpu.VMEM((129 * B, 256), BF),
            pltpu.VMEM((129, B, B), F32),
            pltpu.VMEM((65, B, B), F32),
            pltpu.VMEM((B, B), F32),
            pltpu.VMEM((64, 2, 8, B), F32),
        ],
        compiler_params=pltpu.CompilerParams(vmem_limit_bytes=40 << 20),
        cost_estimate=pl.CostEstimate(
            flops=640 * 2 * 256**3, bytes_accessed=64 << 20, transcendentals=0
        ),
    )(me, signals)


def finish_kernel(me_ref, s_ref, q_ref, b_ref, o_ref, h_ref, l_ref, d_ref, sem):
    parts, rows, own = q_ref.shape
    steps = own // 256

    def send(source, plane, t):
        lanes = pl.ds(own * t, own)
        return pltpu.make_async_copy(source, o_ref.at[plane, :, lanes], sem.at[plane, t])

    copies = [send(q_ref.at[t], 0, t) for t in range(parts)]
    for copy in copies:
        copy.start()
    shape = (4 * B, 256)
    row = lax.broadcasted_iota(jnp.int32, shape, 0)
    col = lax.broadcasted_iota(jnp.int32, shape, 1)
    inner = row % B
    wanted = (inner // 8) * GSIZE + 4 * (row // B) + inner % 8
    spread = jnp.where((inner % 8 < 4) & (col == wanted), 1.0, 0.0).astype(BF)
    tiles = [b_ref[:, pl.ds(8 * u, 8)].astype(F32) for u in range(3)]
    line = lax.broadcasted_iota(jnp.int32, tiles[0].shape, 1)
    chunks = [tiles[0]]
    for t in range(1, parts):
        part = jnp.roll(tiles[t - 1], 2 * t, axis=1)
        if t < parts - 1:
            part = jnp.where(line < 2 * t, part, jnp.roll(tiles[t], 2 * t, axis=1))
        chunks.append(part)
    for t in range(parts):
        chunk = chunks[t].reshape(B * 8, B).astype(BF).T
        for i in range(4):
            for b in range(steps):
                l_ref[pl.ds((t * steps + b) * rows, rows), pl.ds(B * i, B)] = chunk[
                    rows * i : rows * i + rows, B * b : B * b + B
                ]
        span = steps * rows
        grad = jnp.dot(
            l_ref[pl.ds(t * span, span), :], spread, preferred_element_type=F32
        )
        for b in range(steps):
            lanes = pl.ds(own * t + 256 * b, 256)
            here = grad[b * rows : b * rows + rows]
            d_ref[0, :, lanes] = (here * s_ref[2, :, lanes].astype(F32)).astype(BF)
            d_ref[1, :, lanes] = (here * s_ref[1, :, lanes].astype(F32)).astype(BF)
        for plane in (1, 2):
            copy = send(d_ref.at[plane - 1, :, pl.ds(own * t, own)], plane, t)
            copy.start()
            copies.append(copy)
    tail = chunks[0]
    for t in range(1, parts):
        tail = jnp.where(me_ref[0] == t, chunks[t], tail)
    h_ref[...] = jnp.sum(jnp.where((line == 4) | (line == 5), tail, 0.0), axis=1).T
    for copy in copies:
        copy.wait()


def finish(me, saved, d_query, back):
    _, rows, width = saved.shape
    parts, _, own = d_query.shape
    vmem = pl.BlockSpec(memory_space=pltpu.VMEM)
    return pl.pallas_call(
        finish_kernel,
        in_specs=[pl.BlockSpec(memory_space=pltpu.SMEM), vmem, vmem, vmem],
        out_specs=[pl.BlockSpec(memory_space=pl.ANY), vmem],
        out_shape=(
            jax.ShapeDtypeStruct(saved.shape, BF),
            jax.ShapeDtypeStruct((B, own // GSIZE), F32),
        ),
        scratch_shapes=[
            pltpu.VMEM((parts * (own // 256) * rows, 4 * B), BF),
            pltpu.VMEM((2, rows, width), BF),
            pltpu.SemaphoreType.DMA((3, parts)),
        ],
        compiler_params=pltpu.CompilerParams(vmem_limit_bytes=32 << 20),
    )(me, saved, d_query, back)


def swap(x, axis):
    return lax.all_to_all(x, axis, split_axis=0, concat_axis=0, tiled=True)


def shift(chunks, axis):
    size = len(chunks)
    return [chunks[0]] + [
        lax.ppermute(chunks[k], axis, [(i, (i + k) % size) for i in range(size)])
        for k in range(1, size)
    ]


def per_device(saved_rows, grad_out, conv_out, filters):
    saved = saved_rows.transpose(1, 0, 2)
    _, rows, width = saved.shape
    tokens, own = grad_out.shape
    parts = width // own
    groups = own // GSIZE
    me = lax.axis_index("tp").reshape(1)
    *grads, d_query = split(me, grad_out, conv_out, parts)
    spread = pack(me, saved, filters, shift(grads, "tp"))
    spread = spread.reshape(groups * parts, OUT_ROWS // 2, 2, tokens)
    signals, d_query = lax.optimization_barrier((swap(spread, ("ctx", "tp")), d_query))
    home_q = swap(d_query.reshape(parts, rows, own), "tp")
    answer = correlate(me, signals.reshape(groups // 2, 2, parts * OUT_ROWS, tokens))
    answer, home_q = lax.optimization_barrier((answer, home_q))
    back = swap(answer.reshape(groups * parts, BACK_ROWS // 2, 2, tokens), ("ctx", "tp"))
    back = back.reshape(groups, parts * BACK_ROWS, tokens)
    d_saved, d_filters = finish(me, saved, home_q, back)
    return (d_saved.transpose(1, 0, 2), d_filters)


def solution(mesh):
    placed = (P(("ctx", "tp"), None, None), P("ctx", "tp"), P("ctx", "tp"), P("ctx", "tp"))
    return jax.shard_map(
        per_device,
        mesh=mesh,
        in_specs=placed,
        out_specs=(P(("ctx", "tp"), None, None), P("ctx", "tp")),
        check_vma=False,
    )
```

```python
import jax
import jax.numpy as jnp
from jax import lax
from jax.experimental import pallas as pl
from jax.experimental.pallas import tpu as pltpu
from jax.sharding import PartitionSpec as P

GSIZE = 16
B = 128
OUT_ROWS = 10
BACK_ROWS = 6
F32 = jnp.float32
BF = jnp.bfloat16


def split_kernel(me_ref, g_ref, *refs):
    *g_refs, sem = refs
    parts = len(g_refs)
    rows = g_refs[0].shape[0]
    copies = []
    for k, o_ref in enumerate(g_refs):
        at = pl.multiple_of((me_ref[0] + k) % parts * rows, rows)
        copies.append(pltpu.make_async_copy(g_ref.at[pl.ds(at, rows), :], o_ref, sem.at[k]))
    for copy in copies:
        copy.start()
    for copy in copies:
        copy.wait()


def split(me, grad_out, parts):
    tokens, own = grad_out.shape
    vmem = pl.BlockSpec(memory_space=pltpu.VMEM)
    chunk = jax.ShapeDtypeStruct((tokens // parts, own), BF)
    return pl.pallas_call(
        split_kernel,
        in_specs=[
            pl.BlockSpec(memory_space=pltpu.SMEM),
            pl.BlockSpec(memory_space=pl.ANY),
        ],
        out_specs=[vmem] * parts,
        out_shape=[chunk] * parts,
        scratch_shapes=[pltpu.SemaphoreType.DMA((parts,))],
        compiler_params=pltpu.CompilerParams(vmem_limit_bytes=16 << 20),
    )(me, grad_out)


def gather(values, offset, l_ref, store):
    rows, own = values.shape
    steps = own // 256
    shape = (256, 512)
    row = lax.broadcasted_iota(jnp.int32, shape, 0)
    col = lax.broadcasted_iota(jnp.int32, shape, 1)
    wanted = (row % 16) // 4 * B + row // 16 * 8 + offset + row % 4
    weights = jnp.where(col == wanted, 1.0, 0.0).astype(BF)
    for b in range(steps):
        l_ref[pl.ds(b * rows, rows), :] = values[:, 256 * b : 256 * b + 256]
    spread = jnp.dot(l_ref[...], weights, preferred_element_type=F32)
    for b in range(steps):
        here = spread[b * rows : b * rows + rows]
        block = jnp.concatenate([here[:, B * i : B * i + B] for i in range(4)], axis=0)
        store(b, block.T.reshape(16, 8, B))


def prepare_kernel(after_ref, s_ref, g_ref, c_ref, h_ref, q_ref, m_ref, d_ref, t_ref, l_ref):
    del after_ref
    parts = m_ref.shape[0]
    own = g_ref.shape[1]
    q_ref[...] = s_ref[0]
    d_ref[...] = (g_ref[...].astype(F32) * c_ref[...].astype(F32)).astype(BF)
    t_ref[...] = h_ref[...].T
    for t in range(parts):
        lanes = pl.ds(own * t, own)
        mixed = (s_ref[1, :, lanes].astype(F32) * s_ref[2, :, lanes].astype(F32)).astype(BF)

        def store(b, block):
            m_ref[t, pl.ds(16 * b, 16)] = block

        gather(mixed, 4, l_ref, store)


def prepare(after, saved, grad_out, conv_out, filters, parts):
    _, rows, width = saved.shape
    tokens, own = grad_out.shape
    vmem = pl.BlockSpec(memory_space=pltpu.VMEM)
    return pl.pallas_call(
        prepare_kernel,
        in_specs=[pl.BlockSpec(memory_space=pltpu.SMEM)] + [vmem] * 4,
        out_specs=[vmem] * 4,
        out_shape=(
            jax.ShapeDtypeStruct((rows, width), BF),
            jax.ShapeDtypeStruct((parts, B, 8, B), F32),
            jax.ShapeDtypeStruct((tokens, own), BF),
            jax.ShapeDtypeStruct((own // GSIZE, tokens), F32),
        ),
        scratch_shapes=[pltpu.VMEM((own // 256 * rows, 256), BF)],
        compiler_params=pltpu.CompilerParams(vmem_limit_bytes=32 << 20),
        cost_estimate=pl.CostEstimate(
            flops=2 << 30, bytes_accessed=8 << 20, transcendentals=0
        ),
    )(after, saved, grad_out, conv_out, filters)


def pack_kernel(me_ref, s_ref, m_ref, t_ref, *refs):
    *g_refs, o_ref, f_ref, l_ref, c_ref = refs
    parts = len(g_refs)
    rows, own = g_refs[0].shape
    for k, g_ref in enumerate(g_refs):
        source = (me_ref[0] + parts - k) % parts
        f_ref[pl.ds(pl.multiple_of(source * rows, rows), rows), :] = g_ref[...]
    for t in range(parts):
        grad = f_ref[pl.ds(rows * t, rows), :].astype(F32)
        delta = (s_ref[:, pl.ds(own * t, own)].astype(F32) * grad).astype(BF)

        def store(b, block):
            groups = pl.ds(16 * b, 16)
            c_ref[t, groups] = block + m_ref[t, groups]

        gather(delta, 0, l_ref, store)
    shape = (16, 8, B)
    line = lax.broadcasted_iota(jnp.int32, shape, 1)
    for b in range(8):
        groups = pl.ds(16 * b, 16)
        filt = jnp.broadcast_to(t_ref[groups, :][:, None], shape)
        chunks = [c_ref[0, groups]] + [
            jnp.roll(c_ref[t, groups], 2 * t, axis=1) for t in range(1, parts)
        ]
        for u in range(5):
            tile = filt
            if u < parts:
                tile = jnp.where(line >= 2 * u, chunks[u], tile)
            if u > 0:
                tile = jnp.where(line < 2 * u - 2, chunks[u - 1], tile)
            o_ref[groups, pl.ds(8 * u, 8)] = tile.astype(BF)


def pack(me, query, mixed, taps, grads):
    parts = len(grads)
    rows, own = grads[0].shape
    vmem = pl.BlockSpec(memory_space=pltpu.VMEM)
    return pl.pallas_call(
        pack_kernel,
        in_specs=[pl.BlockSpec(memory_space=pltpu.SMEM)] + [vmem] * (3 + parts),
        out_specs=vmem,
        out_shape=jax.ShapeDtypeStruct((own // GSIZE, parts * OUT_ROWS, B), BF),
        scratch_shapes=[
            pltpu.VMEM((parts * rows, own), BF),
            pltpu.VMEM((own // 256 * rows, 256), BF),
            pltpu.VMEM((parts, B, 8, B), F32),
        ],
        compiler_params=pltpu.CompilerParams(vmem_limit_bytes=32 << 20),
    )(me, query, mixed, taps, *grads)


def ungroup(me, x_ref, d_ref, m_ref, n_ref):
    shape = (16, 8, B)
    line = lax.broadcasted_iota(jnp.int32, shape, 1)
    lane = lax.broadcasted_iota(jnp.int32, shape, 2) // 32
    for half in range(2):
        lanes = pl.ds(B * half, B)
        for b in range(4):
            pairs = pl.ds(16 * b, 16)
            tiles = [x_ref[pairs, half, pl.ds(8 * u, 8)].astype(F32) for u in range(5)]
            chunks = [tiles[0]] + [
                jnp.roll(jnp.where(line < 2 * t, tiles[t + 1], tiles[t]), 8 - 2 * t, axis=1)
                for t in range(1, 4)
            ]
            taps = jnp.where((line == 6) | (line == 7), tiles[4], 0.0)
            for t in range(3):
                here = jnp.where((line == 2 * t) | (line == 2 * t + 1), tiles[t + 1], 0.0)
                taps = jnp.where(me == t, here, taps)
            taps = jnp.broadcast_to(0.5 * jnp.sum(taps, axis=1, keepdims=True), shape)
            n_ref[pairs, half] = taps
            turned = []
            for d in range(4):
                mix = chunks[(3 - d) % 4]
                for i in range(3):
                    mix = jnp.where(lane == i, chunks[(i - d) % 4], mix)
                turned.append(mix if d == 0 else jnp.roll(mix, B - 32 * d, axis=2))
            fours = []
            for i in range(4):
                mix = turned[(i - 3) % 4]
                for t in range(3):
                    mix = jnp.where(lane == t, turned[(i - t) % 4], mix)
                fours.append(mix)
            moved = [jnp.roll(x, 4, axis=1) for x in fours]
            top = line < 4
            delta = [jnp.where(top, fours[i], moved[i + 1]) for i in (0, 2)]
            mixed = [jnp.where(top, moved[i], fours[i + 1]) for i in (0, 2)]
            at = pl.ds(256 * b, 256)
            d_ref[at, lanes] = jnp.concatenate(delta, axis=1).reshape(256, B).astype(BF)
            m_ref[at, lanes] = jnp.concatenate(mixed, axis=1).reshape(256, B).astype(BF)


def regroup(part, sums, o_ref, tile, half):
    shape = (16, 8, B)
    row = lax.broadcasted_iota(jnp.int32, shape, 1)
    lane = lax.broadcasted_iota(jnp.int32, shape, 2) // 32
    low, high = part[:, :8], part[:, 8:]
    fours = [low, jnp.roll(low, 4, axis=1), high, jnp.roll(high, 4, axis=1)]
    turned = []
    for d in range(4):
        mix = fours[(3 + d) % 4]
        for t in range(3):
            mix = jnp.where(lane == t, fours[(t + d) % 4], mix)
        turned.append(mix if d == 0 else jnp.roll(mix, 32 * d, axis=2))
    coarse = sums.astype(BF).astype(F32)
    fine = sums - coarse
    coarse = jnp.broadcast_to(coarse[:, None], shape)
    fine = jnp.broadcast_to(fine[:, None], shape)
    rest = jnp.where(row == 4, coarse, jnp.where(row == 5, fine, 0.0))
    chunks = []
    for t in range(4):
        chunk = turned[(3 - t) % 4]
        for i in range(3):
            chunk = jnp.where(lane == i, turned[(i - t) % 4], chunk)
        chunk = jnp.where(row < 4, chunk, rest)
        chunks.append(chunk if t == 0 else jnp.roll(chunk, 8 - 2 * t, axis=1))
    for u in range(3):
        joined = jnp.where(row < 6 - 2 * u, chunks[u], chunks[u + 1])
        o_ref[pl.ds(16 * tile, 16), half, pl.ds(8 * u, 8)] = joined.astype(BF)


def correlate_kernel(
    me_ref, x_ref, o_ref, d_ref, m_ref, t_ref, f_ref, w_ref, qa_ref, qb_ref, l_ref, n_ref
):
    ungroup(me_ref[0], x_ref, d_ref, m_ref, n_ref)
    d_ref[pl.ds(1024, 256), :] = jnp.zeros((256, 256), BF)
    row = lax.broadcasted_iota(jnp.int32, (B, B), 0)
    col = lax.broadcasted_iota(jnp.int32, (B, B), 1)

    flip = jnp.where((row + col) % B == 0, 1.0, 0.0).astype(BF)
    taps = n_ref[...].reshape(1024, B).astype(BF)
    f_ref[...] = jnp.dot(taps, flip, preferred_element_type=F32).reshape(B, 8, B)
    lower = row >= col
    w_ref[pl.ds(0, B), pl.ds(B, B)] = jnp.zeros((B, B), BF)

    def build(e, before):
        line = jnp.broadcast_to(f_ref[pl.ds(e, 1)], (16, 8, B)).reshape(B, B)
        turned = pltpu.roll(line, 0, 1, stride=1, stride_axis=0)
        block = jnp.where(lower, turned, before).astype(BF)
        at = pl.multiple_of(e * B, B)
        w_ref[pl.ds(at, B), pl.ds(0, B)] = block
        w_ref[pl.ds(at + B, B), pl.ds(B, B)] = block
        return turned

    before = jnp.zeros((B, B), F32)
    mirror = jnp.where(row + col == B - 1, 1.0, 0.0).astype(BF)
    for half in range(2):
        t_ref[pl.ds(B * half, B), :] = lax.dot_general(
            mirror,
            m_ref[:, pl.ds(B * half, B)],
            (((1,), (1,)), ((), ())),
            preferred_element_type=F32,
        ).astype(BF)
    for part in range(4):
        depth = 256 * (4 - part)

        def gram(k, carry):
            e = 16 * part + k
            table = jnp.dot(
                t_ref[:, pl.ds(0, depth)],
                d_ref[pl.ds(pl.multiple_of(16 * e, 16), depth), :],
                preferred_element_type=F32,
            )
            qa_ref[2 * e] = table[:B, :B] + table[B:, B:]
            qa_ref[2 * e + 1] = table[:B, B:]
            qb_ref[e] = table[B:, :B]
            return build(2 * e + 1, build(2 * e, carry))

        before = lax.fori_loop(0, 16, gram, before, unroll=16)
    qb_ref[64] = jnp.zeros((B, B), F32)
    qa_ref[128] = jnp.zeros((B, B), F32)
    keep = row + col >= B - 1

    def diagonals(e, carry):
        first = qa_ref[2 * e]
        second = qa_ref[2 * e + 1] + qb_ref[e + 1]
        third = qa_ref[2 * e + 2]
        for u, (here, ahead) in enumerate(((first, second), (second, third))):
            turned = pltpu.roll(jnp.where(keep, here, ahead), 1, 1, stride=1, stride_axis=0)
            l_ref[pl.ds(2 * e + u, 1), :] = jnp.sum(turned, axis=0, keepdims=True)
        return carry

    for tile in range(4):
        count = 64 - 16 * tile
        left = jnp.concatenate(
            [d_ref[pl.ds(256 * tile + 16 * u, 256), :] for u in range(count)], axis=1
        )
        total = jnp.dot(left, w_ref[pl.ds(0, 256 * count), :], preferred_element_type=F32)
        for e in range(16 * tile, 16 * tile + 16):
            diagonals(e, 0)
        for half in range(2):
            part = total[:, B * half : B * half + B].reshape(16, GSIZE, B)
            sums = l_ref[pl.ds(32 * tile + half, 16, stride=2), :]
            regroup(part, sums, o_ref, tile, half)


def correlate(me, signals):
    return pl.pallas_call(
        correlate_kernel,
        in_specs=[
            pl.BlockSpec(memory_space=pltpu.SMEM),
            pl.BlockSpec(memory_space=pltpu.VMEM),
        ],
        out_specs=pl.BlockSpec(memory_space=pltpu.VMEM),
        out_shape=jax.ShapeDtypeStruct((64, 2, 4 * BACK_ROWS, B), BF),
        scratch_shapes=[
            pltpu.VMEM((1280, 256), BF),
            pltpu.VMEM((1024, 256), BF),
            pltpu.VMEM((256, 1024), BF),
            pltpu.VMEM((B, 8, B), F32),
            pltpu.VMEM((129 * B, 256), BF),
            pltpu.VMEM((129, B, B), F32),
            pltpu.VMEM((65, B, B), F32),
            pltpu.VMEM((B, B), F32),
            pltpu.VMEM((64, 2, 8, B), F32),
        ],
        compiler_params=pltpu.CompilerParams(vmem_limit_bytes=40 << 20),
        cost_estimate=pl.CostEstimate(
            flops=640 * 2 * 256**3, bytes_accessed=64 << 20, transcendentals=0
        ),
    )(me, signals)


def finish_kernel(me_ref, s_ref, q_ref, b_ref, o_ref, h_ref, l_ref, d_ref, sem):
    parts, rows, own = q_ref.shape
    steps = own // 256

    def send(source, plane, t):
        lanes = pl.ds(own * t, own)
        return pltpu.make_async_copy(source, o_ref.at[plane, :, lanes], sem.at[plane, t])

    copies = [send(q_ref.at[t], 0, t) for t in range(parts)]
    for copy in copies:
        copy.start()
    shape = (4 * B, 256)
    row = lax.broadcasted_iota(jnp.int32, shape, 0)
    col = lax.broadcasted_iota(jnp.int32, shape, 1)
    inner = row % B
    wanted = (inner // 8) * GSIZE + 4 * (row // B) + inner % 8
    spread = jnp.where((inner % 8 < 4) & (col == wanted), 1.0, 0.0).astype(BF)
    tiles = [b_ref[:, pl.ds(8 * u, 8)].astype(F32) for u in range(3)]
    line = lax.broadcasted_iota(jnp.int32, tiles[0].shape, 1)
    chunks = [tiles[0]]
    for t in range(1, parts):
        part = jnp.roll(tiles[t - 1], 2 * t, axis=1)
        if t < parts - 1:
            part = jnp.where(line < 2 * t, part, jnp.roll(tiles[t], 2 * t, axis=1))
        chunks.append(part)
    for t in range(parts):
        chunk = chunks[t].reshape(B * 8, B).astype(BF).T
        for i in range(4):
            for b in range(steps):
                l_ref[pl.ds((t * steps + b) * rows, rows), pl.ds(B * i, B)] = chunk[
                    rows * i : rows * i + rows, B * b : B * b + B
                ]
        span = steps * rows
        grad = jnp.dot(
            l_ref[pl.ds(t * span, span), :], spread, preferred_element_type=F32
        )
        for b in range(steps):
            lanes = pl.ds(own * t + 256 * b, 256)
            here = grad[b * rows : b * rows + rows]
            d_ref[0, :, lanes] = (here * s_ref[2, :, lanes].astype(F32)).astype(BF)
            d_ref[1, :, lanes] = (here * s_ref[1, :, lanes].astype(F32)).astype(BF)
        for plane in (1, 2):
            copy = send(d_ref.at[plane - 1, :, pl.ds(own * t, own)], plane, t)
            copy.start()
            copies.append(copy)
    tail = chunks[0]
    for t in range(1, parts):
        tail = jnp.where(me_ref[0] == t, chunks[t], tail)
    h_ref[...] = jnp.sum(jnp.where((line == 4) | (line == 5), tail, 0.0), axis=1).T
    for copy in copies:
        copy.wait()


def finish(me, saved, d_query, back):
    _, rows, width = saved.shape
    parts, _, own = d_query.shape
    vmem = pl.BlockSpec(memory_space=pltpu.VMEM)
    return pl.pallas_call(
        finish_kernel,
        in_specs=[pl.BlockSpec(memory_space=pltpu.SMEM), vmem, vmem, vmem],
        out_specs=[pl.BlockSpec(memory_space=pl.ANY), vmem],
        out_shape=(
            jax.ShapeDtypeStruct(saved.shape, BF),
            jax.ShapeDtypeStruct((B, own // GSIZE), F32),
        ),
        scratch_shapes=[
            pltpu.VMEM((parts * (own // 256) * rows, 4 * B), BF),
            pltpu.VMEM((2, rows, width), BF),
            pltpu.SemaphoreType.DMA((3, parts)),
        ],
        compiler_params=pltpu.CompilerParams(vmem_limit_bytes=32 << 20),
    )(me, saved, d_query, back)


def swap(x, axis):
    return lax.all_to_all(x, axis, split_axis=0, concat_axis=0, tiled=True)


def shift(chunks, axis):
    size = len(chunks)
    return [chunks[0]] + [
        lax.ppermute(chunks[k], axis, [(i, (i + k) % size) for i in range(size)])
        for k in range(1, size)
    ]


def per_device(saved_rows, grad_out, conv_out, filters):
    saved = saved_rows.transpose(1, 0, 2)
    _, rows, width = saved.shape
    tokens, own = grad_out.shape
    parts = width // own
    groups = own // GSIZE
    me = lax.axis_index("tp").reshape(1)
    *grads, after = lax.optimization_barrier((*split(me, grad_out, parts), me))
    query, mixed, d_query, taps = prepare(after, saved, grad_out, conv_out, filters, parts)
    spread = pack(me, query, mixed, taps, shift(grads, "tp"))
    spread = spread.reshape(groups * parts, OUT_ROWS // 2, 2, tokens)
    signals, d_query = lax.optimization_barrier((swap(spread, ("ctx", "tp")), d_query))
    home_q = swap(d_query.reshape(parts, rows, own), "tp")
    answer = correlate(me, signals.reshape(groups // 2, 2, parts * OUT_ROWS, tokens))
    answer, home_q = lax.optimization_barrier((answer, home_q))
    back = swap(answer.reshape(groups * parts, BACK_ROWS // 2, 2, tokens), ("ctx", "tp"))
    back = back.reshape(groups, parts * BACK_ROWS, tokens)
    d_saved, d_filters = finish(me, saved, home_q, back)
    return (d_saved.transpose(1, 0, 2), d_filters)


def solution(mesh):
    placed = (P(("ctx", "tp"), None, None), P("ctx", "tp"), P("ctx", "tp"), P("ctx", "tp"))
    return jax.shard_map(
        per_device,
        mesh=mesh,
        in_specs=placed,
        out_specs=(P(("ctx", "tp"), None, None), P("ctx", "tp")),
        check_vma=False,
    )
```

```python
import jax
import jax.numpy as jnp
from jax import lax
from jax.experimental import pallas as pl
from jax.experimental.pallas import tpu as pltpu
from jax.sharding import Mesh
from jax.sharding import PartitionSpec as P

GSIZE = 16
B = 128
OUT_ROWS = 10
BACK_ROWS = 6
CTX = {"y": 8, "zh": 2, "x": 4, "core": 2}
ORDER = ("x", "core", "y", "zh", "tp")
F32 = jnp.float32
BF = jnp.bfloat16


def split_kernel(me_ref, g_ref, *refs):
    *g_refs, sem = refs
    parts = len(g_refs)
    rows = g_refs[0].shape[0]
    copies = []
    for k, o_ref in enumerate(g_refs):
        at = pl.multiple_of((me_ref[0] + k) % parts * rows, rows)
        copies.append(pltpu.make_async_copy(g_ref.at[pl.ds(at, rows), :], o_ref, sem.at[k]))
    for copy in copies:
        copy.start()
    for copy in copies:
        copy.wait()


def split(me, grad_out, parts):
    tokens, own = grad_out.shape
    vmem = pl.BlockSpec(memory_space=pltpu.VMEM)
    chunk = jax.ShapeDtypeStruct((tokens // parts, own), BF)
    return pl.pallas_call(
        split_kernel,
        in_specs=[
            pl.BlockSpec(memory_space=pltpu.SMEM),
            pl.BlockSpec(memory_space=pl.ANY),
        ],
        out_specs=[vmem] * parts,
        out_shape=[chunk] * parts,
        scratch_shapes=[pltpu.SemaphoreType.DMA((parts,))],
        compiler_params=pltpu.CompilerParams(vmem_limit_bytes=16 << 20),
    )(me, grad_out)


def gather(values, offset, l_ref, store):
    rows, own = values.shape
    steps = own // 256
    shape = (256, 512)
    row = lax.broadcasted_iota(jnp.int32, shape, 0)
    col = lax.broadcasted_iota(jnp.int32, shape, 1)
    wanted = (row % 16) // 4 * B + row // 16 * 8 + offset + row % 4
    weights = jnp.where(col == wanted, 1.0, 0.0).astype(BF)
    for b in range(steps):
        l_ref[pl.ds(b * rows, rows), :] = values[:, 256 * b : 256 * b + 256]
    spread = jnp.dot(l_ref[...], weights, preferred_element_type=F32)
    for b in range(steps):
        here = spread[b * rows : b * rows + rows]
        block = jnp.concatenate([here[:, B * i : B * i + B] for i in range(4)], axis=0)
        store(b, block.T.reshape(16, 8, B))


def prepare_kernel(after_ref, s_ref, g_ref, c_ref, h_ref, q_ref, m_ref, d_ref, t_ref, l_ref):
    del after_ref
    parts = m_ref.shape[0]
    own = g_ref.shape[1]
    q_ref[...] = s_ref[0]
    d_ref[...] = (g_ref[...].astype(F32) * c_ref[...].astype(F32)).astype(BF)
    t_ref[...] = h_ref[...].T
    for t in range(parts):
        lanes = pl.ds(own * t, own)
        mixed = (s_ref[1, :, lanes].astype(F32) * s_ref[2, :, lanes].astype(F32)).astype(BF)

        def store(b, block):
            m_ref[t, pl.ds(16 * b, 16)] = block

        gather(mixed, 4, l_ref, store)


def prepare(after, saved, grad_out, conv_out, filters, parts):
    _, rows, width = saved.shape
    tokens, own = grad_out.shape
    vmem = pl.BlockSpec(memory_space=pltpu.VMEM)
    return pl.pallas_call(
        prepare_kernel,
        in_specs=[pl.BlockSpec(memory_space=pltpu.SMEM)] + [vmem] * 4,
        out_specs=[vmem] * 4,
        out_shape=(
            jax.ShapeDtypeStruct((rows, width), BF),
            jax.ShapeDtypeStruct((parts, B, 8, B), F32),
            jax.ShapeDtypeStruct((tokens, own), BF),
            jax.ShapeDtypeStruct((own // GSIZE, tokens), F32),
        ),
        scratch_shapes=[pltpu.VMEM((own // 256 * rows, 256), BF)],
        compiler_params=pltpu.CompilerParams(vmem_limit_bytes=32 << 20),
        cost_estimate=pl.CostEstimate(
            flops=2 << 30, bytes_accessed=8 << 20, transcendentals=0
        ),
    )(after, saved, grad_out, conv_out, filters)


def pack_kernel(me_ref, s_ref, m_ref, t_ref, *refs):
    *g_refs, o_ref, f_ref, l_ref, c_ref = refs
    parts = len(g_refs)
    rows, own = g_refs[0].shape
    for k, g_ref in enumerate(g_refs):
        source = (me_ref[0] + parts - k) % parts
        f_ref[pl.ds(pl.multiple_of(source * rows, rows), rows), :] = g_ref[...]
    for t in range(parts):
        grad = f_ref[pl.ds(rows * t, rows), :].astype(F32)
        delta = (s_ref[:, pl.ds(own * t, own)].astype(F32) * grad).astype(BF)

        def store(b, block):
            groups = pl.ds(16 * b, 16)
            c_ref[t, groups] = block + m_ref[t, groups]

        gather(delta, 0, l_ref, store)
    shape = (16, 8, B)
    line = lax.broadcasted_iota(jnp.int32, shape, 1)
    for b in range(8):
        groups = pl.ds(16 * b, 16)
        filt = jnp.broadcast_to(t_ref[groups, :][:, None], shape)
        chunks = [c_ref[0, groups]] + [
            jnp.roll(c_ref[t, groups], 2 * t, axis=1) for t in range(1, parts)
        ]
        for u in range(5):
            tile = filt
            if u < parts:
                tile = jnp.where(line >= 2 * u, chunks[u], tile)
            if u > 0:
                tile = jnp.where(line < 2 * u - 2, chunks[u - 1], tile)
            tile = tile.astype(BF).reshape(2, 4, 2, 8, B)
            for x in range(4):
                for core in range(2):
                    o_ref[x, core, b, :, pl.ds(8 * u, 8)] = tile[:, x, core]


def pack(me, query, mixed, taps, grads):
    parts = len(grads)
    rows, own = grads[0].shape
    vmem = pl.BlockSpec(memory_space=pltpu.VMEM)
    return pl.pallas_call(
        pack_kernel,
        in_specs=[pl.BlockSpec(memory_space=pltpu.SMEM)] + [vmem] * (3 + parts),
        out_specs=vmem,
        out_shape=jax.ShapeDtypeStruct((4, 2, 8, 2, parts * OUT_ROWS, B), BF),
        scratch_shapes=[
            pltpu.VMEM((parts * rows, own), BF),
            pltpu.VMEM((own // 256 * rows, 256), BF),
            pltpu.VMEM((parts, B, 8, B), F32),
        ],
        compiler_params=pltpu.CompilerParams(vmem_limit_bytes=32 << 20),
    )(me, query, mixed, taps, *grads)


def ungroup(me, x_ref, d_ref, m_ref, n_ref):
    shape = (16, 8, B)
    line = lax.broadcasted_iota(jnp.int32, shape, 1)
    lane = lax.broadcasted_iota(jnp.int32, shape, 2) // 32
    for half in range(2):
        lanes = pl.ds(B * half, B)
        for b in range(4):
            pairs = pl.ds(16 * b, 16)
            tiles = [
                jnp.stack(
                    [x_ref[x, half, pl.ds(2 * b, 2), :, pl.ds(8 * u, 8)] for x in range(4)], axis=2
                )
                .reshape(shape)
                .astype(F32)
                for u in range(5)
            ]
            chunks = [tiles[0]] + [
                jnp.roll(jnp.where(line < 2 * t, tiles[t + 1], tiles[t]), 8 - 2 * t, axis=1)
                for t in range(1, 4)
            ]
            taps = jnp.where((line == 6) | (line == 7), tiles[4], 0.0)
            for t in range(3):
                here = jnp.where((line == 2 * t) | (line == 2 * t + 1), tiles[t + 1], 0.0)
                taps = jnp.where(me == t, here, taps)
            taps = jnp.broadcast_to(0.5 * jnp.sum(taps, axis=1, keepdims=True), shape)
            n_ref[pairs, half] = taps
            turned = []
            for d in range(4):
                mix = chunks[(3 - d) % 4]
                for i in range(3):
                    mix = jnp.where(lane == i, chunks[(i - d) % 4], mix)
                turned.append(mix if d == 0 else jnp.roll(mix, B - 32 * d, axis=2))
            fours = []
            for i in range(4):
                mix = turned[(i - 3) % 4]
                for t in range(3):
                    mix = jnp.where(lane == t, turned[(i - t) % 4], mix)
                fours.append(mix)
            moved = [jnp.roll(x, 4, axis=1) for x in fours]
            top = line < 4
            delta = [jnp.where(top, fours[i], moved[i + 1]) for i in (0, 2)]
            mixed = [jnp.where(top, moved[i], fours[i + 1]) for i in (0, 2)]
            at = pl.ds(256 * b, 256)
            d_ref[at, lanes] = jnp.concatenate(delta, axis=1).reshape(256, B).astype(BF)
            m_ref[at, lanes] = jnp.concatenate(mixed, axis=1).reshape(256, B).astype(BF)


def regroup(part, sums, o_ref, tile, half):
    shape = (16, 8, B)
    row = lax.broadcasted_iota(jnp.int32, shape, 1)
    lane = lax.broadcasted_iota(jnp.int32, shape, 2) // 32
    low, high = part[:, :8], part[:, 8:]
    fours = [low, jnp.roll(low, 4, axis=1), high, jnp.roll(high, 4, axis=1)]
    turned = []
    for d in range(4):
        mix = fours[(3 + d) % 4]
        for t in range(3):
            mix = jnp.where(lane == t, fours[(t + d) % 4], mix)
        turned.append(mix if d == 0 else jnp.roll(mix, 32 * d, axis=2))
    coarse = sums.astype(BF).astype(F32)
    fine = sums - coarse
    coarse = jnp.broadcast_to(coarse[:, None], shape)
    fine = jnp.broadcast_to(fine[:, None], shape)
    rest = jnp.where(row == 4, coarse, jnp.where(row == 5, fine, 0.0))
    chunks = []
    for t in range(4):
        chunk = turned[(3 - t) % 4]
        for i in range(3):
            chunk = jnp.where(lane == i, turned[(i - t) % 4], chunk)
        chunk = jnp.where(row < 4, chunk, rest)
        chunks.append(chunk if t == 0 else jnp.roll(chunk, 8 - 2 * t, axis=1))
    for u in range(3):
        joined = jnp.where(row < 6 - 2 * u, chunks[u], chunks[u + 1])
        joined = joined.astype(BF).reshape(2, 2, 4, 8, B)
        for x in range(4):
            o_ref[x, half, pl.ds(2 * tile, 2), :, pl.ds(8 * u, 8)] = joined[:, :, x]


def correlate_kernel(
    me_ref, x_ref, o_ref, d_ref, m_ref, t_ref, f_ref, w_ref, qa_ref, qb_ref, l_ref, n_ref
):
    ungroup(me_ref[0], x_ref, d_ref, m_ref, n_ref)
    d_ref[pl.ds(1024, 256), :] = jnp.zeros((256, 256), BF)
    row = lax.broadcasted_iota(jnp.int32, (B, B), 0)
    col = lax.broadcasted_iota(jnp.int32, (B, B), 1)

    flip = jnp.where((row + col) % B == 0, 1.0, 0.0).astype(BF)
    taps = n_ref[...].reshape(1024, B).astype(BF)
    f_ref[...] = jnp.dot(taps, flip, preferred_element_type=F32).reshape(B, 8, B)
    lower = row >= col
    w_ref[pl.ds(0, B), pl.ds(B, B)] = jnp.zeros((B, B), BF)

    def build(e, before):
        line = jnp.broadcast_to(f_ref[pl.ds(e, 1)], (16, 8, B)).reshape(B, B)
        turned = pltpu.roll(line, 0, 1, stride=1, stride_axis=0)
        block = jnp.where(lower, turned, before).astype(BF)
        at = pl.multiple_of(e * B, B)
        w_ref[pl.ds(at, B), pl.ds(0, B)] = block
        w_ref[pl.ds(at + B, B), pl.ds(B, B)] = block
        return turned

    before = jnp.zeros((B, B), F32)
    mirror = jnp.where(row + col == B - 1, 1.0, 0.0).astype(BF)
    for half in range(2):
        t_ref[pl.ds(B * half, B), :] = lax.dot_general(
            mirror,
            m_ref[:, pl.ds(B * half, B)],
            (((1,), (1,)), ((), ())),
            preferred_element_type=F32,
        ).astype(BF)
    for part in range(4):
        depth = 256 * (4 - part)

        def gram(k, carry):
            e = 16 * part + k
            table = jnp.dot(
                t_ref[:, pl.ds(0, depth)],
                d_ref[pl.ds(pl.multiple_of(16 * e, 16), depth), :],
                preferred_element_type=F32,
            )
            qa_ref[2 * e] = table[:B, :B] + table[B:, B:]
            qa_ref[2 * e + 1] = table[:B, B:]
            qb_ref[e] = table[B:, :B]
            return build(2 * e + 1, build(2 * e, carry))

        before = lax.fori_loop(0, 16, gram, before, unroll=16)
    qb_ref[64] = jnp.zeros((B, B), F32)
    qa_ref[128] = jnp.zeros((B, B), F32)
    keep = row + col >= B - 1

    def diagonals(e, carry):
        first = qa_ref[2 * e]
        second = qa_ref[2 * e + 1] + qb_ref[e + 1]
        third = qa_ref[2 * e + 2]
        for u, (here, ahead) in enumerate(((first, second), (second, third))):
            turned = pltpu.roll(jnp.where(keep, here, ahead), 1, 1, stride=1, stride_axis=0)
            l_ref[pl.ds(2 * e + u, 1), :] = jnp.sum(turned, axis=0, keepdims=True)
        return carry

    for tile in range(4):
        count = 64 - 16 * tile
        left = jnp.concatenate(
            [d_ref[pl.ds(256 * tile + 16 * u, 256), :] for u in range(count)], axis=1
        )
        total = jnp.dot(left, w_ref[pl.ds(0, 256 * count), :], preferred_element_type=F32)
        for e in range(16 * tile, 16 * tile + 16):
            diagonals(e, 0)
        for half in range(2):
            part = total[:, B * half : B * half + B].reshape(16, GSIZE, B)
            sums = l_ref[pl.ds(32 * tile + half, 16, stride=2), :]
            regroup(part, sums, o_ref, tile, half)


def correlate(me, signals):
    return pl.pallas_call(
        correlate_kernel,
        in_specs=[
            pl.BlockSpec(memory_space=pltpu.SMEM),
            pl.BlockSpec(memory_space=pltpu.VMEM),
        ],
        out_specs=pl.BlockSpec(memory_space=pltpu.VMEM),
        out_shape=jax.ShapeDtypeStruct((4, 2, 8, 2, 4 * BACK_ROWS, B), BF),
        scratch_shapes=[
            pltpu.VMEM((1280, 256), BF),
            pltpu.VMEM((1024, 256), BF),
            pltpu.VMEM((256, 1024), BF),
            pltpu.VMEM((B, 8, B), F32),
            pltpu.VMEM((129 * B, 256), BF),
            pltpu.VMEM((129, B, B), F32),
            pltpu.VMEM((65, B, B), F32),
            pltpu.VMEM((B, B), F32),
            pltpu.VMEM((64, 2, 8, B), F32),
        ],
        compiler_params=pltpu.CompilerParams(vmem_limit_bytes=40 << 20),
        cost_estimate=pl.CostEstimate(
            flops=640 * 2 * 256**3, bytes_accessed=64 << 20, transcendentals=0
        ),
    )(me, signals)


def finish_kernel(me_ref, s_ref, q_ref, b_ref, o_ref, h_ref, l_ref, d_ref, sem):
    parts, rows, own = q_ref.shape
    steps = own // 256

    def send(source, plane, t):
        lanes = pl.ds(own * t, own)
        return pltpu.make_async_copy(source, o_ref.at[plane, :, lanes], sem.at[plane, t])

    copies = [send(q_ref.at[t], 0, t) for t in range(parts)]
    for copy in copies:
        copy.start()
    shape = (4 * B, 256)
    row = lax.broadcasted_iota(jnp.int32, shape, 0)
    col = lax.broadcasted_iota(jnp.int32, shape, 1)
    inner = row % B
    wanted = (inner // 8) * GSIZE + 4 * (row // B) + inner % 8
    spread = jnp.where((inner % 8 < 4) & (col == wanted), 1.0, 0.0).astype(BF)
    tiles = [
        jnp.stack(
            [
                jnp.stack([b_ref[x, core, :, :, pl.ds(8 * u, 8)] for core in range(2)], axis=2)
                for x in range(4)
            ],
            axis=2,
        )
        .reshape(B, 8, B)
        .astype(F32)
        for u in range(3)
    ]
    line = lax.broadcasted_iota(jnp.int32, tiles[0].shape, 1)
    chunks = [tiles[0]]
    for t in range(1, parts):
        part = jnp.roll(tiles[t - 1], 2 * t, axis=1)
        if t < parts - 1:
            part = jnp.where(line < 2 * t, part, jnp.roll(tiles[t], 2 * t, axis=1))
        chunks.append(part)
    for t in range(parts):
        chunk = chunks[t].reshape(B * 8, B).astype(BF).T
        for i in range(4):
            for b in range(steps):
                l_ref[pl.ds((t * steps + b) * rows, rows), pl.ds(B * i, B)] = chunk[
                    rows * i : rows * i + rows, B * b : B * b + B
                ]
        span = steps * rows
        grad = jnp.dot(
            l_ref[pl.ds(t * span, span), :], spread, preferred_element_type=F32
        )
        for b in range(steps):
            lanes = pl.ds(own * t + 256 * b, 256)
            here = grad[b * rows : b * rows + rows]
            d_ref[0, :, lanes] = (here * s_ref[2, :, lanes].astype(F32)).astype(BF)
            d_ref[1, :, lanes] = (here * s_ref[1, :, lanes].astype(F32)).astype(BF)
        for plane in (1, 2):
            copy = send(d_ref.at[plane - 1, :, pl.ds(own * t, own)], plane, t)
            copy.start()
            copies.append(copy)
    tail = chunks[0]
    for t in range(1, parts):
        tail = jnp.where(me_ref[0] == t, chunks[t], tail)
    h_ref[...] = jnp.sum(jnp.where((line == 4) | (line == 5), tail, 0.0), axis=1).T
    for copy in copies:
        copy.wait()


def finish(me, saved, d_query, back):
    _, rows, width = saved.shape
    parts, _, own = d_query.shape
    vmem = pl.BlockSpec(memory_space=pltpu.VMEM)
    return pl.pallas_call(
        finish_kernel,
        in_specs=[pl.BlockSpec(memory_space=pltpu.SMEM), vmem, vmem, vmem],
        out_specs=[pl.BlockSpec(memory_space=pl.ANY), vmem],
        out_shape=(
            jax.ShapeDtypeStruct(saved.shape, BF),
            jax.ShapeDtypeStruct((B, own // GSIZE), F32),
        ),
        scratch_shapes=[
            pltpu.VMEM((parts * (own // 256) * rows, 4 * B), BF),
            pltpu.VMEM((2, rows, width), BF),
            pltpu.SemaphoreType.DMA((3, parts)),
        ],
        compiler_params=pltpu.CompilerParams(vmem_limit_bytes=32 << 20),
    )(me, saved, d_query, back)


def swap(x, axis):
    return lax.all_to_all(x, axis, split_axis=0, concat_axis=0, tiled=True)


def shift(chunks, axis):
    size = len(chunks)
    return [chunks[0]] + [
        lax.ppermute(chunks[k], axis, [(i, (i + k) % size) for i in range(size)])
        for k in range(1, size)
    ]


def per_device(saved_rows, grad_out, conv_out, filters):
    saved = saved_rows.transpose(1, 0, 2)
    _, rows, width = saved.shape
    tokens, own = grad_out.shape
    parts = width // own
    groups = own // GSIZE
    me = lax.axis_index("tp").reshape(1)
    *grads, after = lax.optimization_barrier((*split(me, grad_out, parts), me))
    query, mixed, d_query, taps = prepare(after, saved, grad_out, conv_out, filters, parts)
    spread = pack(me, query, mixed, taps, shift(grads, "tp"))
    spread = spread.reshape(groups * parts, OUT_ROWS // 2, 2, tokens)
    signals, d_query = lax.optimization_barrier((swap(spread, ORDER), d_query))
    home_q = swap(d_query.reshape(parts, rows, own), "tp")
    answer = correlate(me, signals.reshape(4, 2, 8, 2, parts * OUT_ROWS, tokens))
    answer, home_q = lax.optimization_barrier((answer, home_q))
    back = swap(answer.reshape(groups * parts, BACK_ROWS // 2, 2, tokens), ORDER)
    back = back.reshape(4, 2, 8, 2, parts * BACK_ROWS, tokens)
    d_saved, d_filters = finish(me, saved, home_q, back)
    return (d_saved.transpose(1, 0, 2), d_filters)


def solution(mesh):
    names = tuple(CTX) + ("tp",)
    split_mesh = Mesh(mesh.devices.reshape(*CTX.values(), -1), names)
    ctx = tuple(CTX)
    placed = (P(names, None, None), P(ctx, "tp"), P(ctx, "tp"), P(ctx, "tp"))
    return jax.shard_map(
        per_device,
        mesh=split_mesh,
        in_specs=placed,
        out_specs=(P(names, None, None), P(ctx, "tp")),
        check_vma=False,
    )
```

```python
import jax
import jax.numpy as jnp
from jax import lax
from jax.experimental import pallas as pl
from jax.experimental.pallas import tpu as pltpu
from jax.sharding import PartitionSpec as P

GSIZE = 16
B = 128
OUT_ROWS = 10
BACK_ROWS = 6
F32 = jnp.float32
BF = jnp.bfloat16


def gather(values, offset, l_ref, store):
    rows, own = values.shape
    steps = own // 256
    shape = (256, 512)
    row = lax.broadcasted_iota(jnp.int32, shape, 0)
    col = lax.broadcasted_iota(jnp.int32, shape, 1)
    wanted = (row % 16) // 4 * B + row // 16 * 8 + offset + row % 4
    weights = jnp.where(col == wanted, 1.0, 0.0).astype(BF)
    for b in range(steps):
        l_ref[pl.ds(b * rows, rows), :] = values[:, 256 * b : 256 * b + 256]
    spread = jnp.dot(l_ref[...], weights, preferred_element_type=F32)
    for b in range(steps):
        here = spread[b * rows : b * rows + rows]
        block = jnp.concatenate([here[:, B * i : B * i + B] for i in range(4)], axis=0)
        store(b, block.T.reshape(16, 8, B))


def prepare_kernel(after_ref, s_ref, g_ref, c_ref, h_ref, q_ref, m_ref, d_ref, t_ref, l_ref):
    del after_ref
    parts = m_ref.shape[0]
    own = g_ref.shape[1]
    q_ref[...] = s_ref[0]
    d_ref[...] = (g_ref[...].astype(F32) * c_ref[...].astype(F32)).astype(BF)
    t_ref[...] = h_ref[...].T
    for t in range(parts):
        lanes = pl.ds(own * t, own)
        mixed = (s_ref[1, :, lanes].astype(F32) * s_ref[2, :, lanes].astype(F32)).astype(BF)

        def store(b, block):
            m_ref[t, pl.ds(16 * b, 16)] = block

        gather(mixed, 4, l_ref, store)


def prepare(after, saved, grad_out, conv_out, filters, parts):
    _, rows, width = saved.shape
    tokens, own = grad_out.shape
    vmem = pl.BlockSpec(memory_space=pltpu.VMEM)
    return pl.pallas_call(
        prepare_kernel,
        in_specs=[pl.BlockSpec(memory_space=pltpu.SMEM)] + [vmem] * 4,
        out_specs=[vmem] * 4,
        out_shape=(
            jax.ShapeDtypeStruct((rows, width), BF),
            jax.ShapeDtypeStruct((parts, B, 8, B), F32),
            jax.ShapeDtypeStruct((tokens, own), BF),
            jax.ShapeDtypeStruct((own // GSIZE, tokens), F32),
        ),
        scratch_shapes=[pltpu.VMEM((own // 256 * rows, 256), BF)],
        compiler_params=pltpu.CompilerParams(vmem_limit_bytes=32 << 20),
        cost_estimate=pl.CostEstimate(
            flops=2 << 30, bytes_accessed=8 << 20, transcendentals=0
        ),
    )(after, saved, grad_out, conv_out, filters)


def pack_kernel(me_ref, s_ref, m_ref, t_ref, *refs):
    *g_refs, o_ref, f_ref, l_ref, c_ref = refs
    parts = len(g_refs)
    rows, own = g_refs[0].shape
    for k, g_ref in enumerate(g_refs):
        source = (me_ref[0] + parts - k) % parts
        f_ref[pl.ds(pl.multiple_of(source * rows, rows), rows), :] = g_ref[...]
    for t in range(parts):
        grad = f_ref[pl.ds(rows * t, rows), :].astype(F32)
        delta = (s_ref[:, pl.ds(own * t, own)].astype(F32) * grad).astype(BF)

        def store(b, block):
            groups = pl.ds(16 * b, 16)
            c_ref[t, groups] = block + m_ref[t, groups]

        gather(delta, 0, l_ref, store)
    shape = (16, 8, B)
    line = lax.broadcasted_iota(jnp.int32, shape, 1)
    for b in range(8):
        groups = pl.ds(16 * b, 16)
        filt = jnp.broadcast_to(t_ref[groups, :][:, None], shape)
        chunks = [c_ref[0, groups]] + [
            jnp.roll(c_ref[t, groups], 2 * t, axis=1) for t in range(1, parts)
        ]
        for u in range(5):
            tile = filt
            if u < parts:
                tile = jnp.where(line >= 2 * u, chunks[u], tile)
            if u > 0:
                tile = jnp.where(line < 2 * u - 2, chunks[u - 1], tile)
            o_ref[groups, pl.ds(8 * u, 8)] = tile.astype(BF)


def pack(me, query, mixed, taps, grads):
    parts = len(grads)
    rows, own = grads[0].shape
    vmem = pl.BlockSpec(memory_space=pltpu.VMEM)
    return pl.pallas_call(
        pack_kernel,
        in_specs=[pl.BlockSpec(memory_space=pltpu.SMEM)] + [vmem] * (3 + parts),
        out_specs=vmem,
        out_shape=jax.ShapeDtypeStruct((own // GSIZE, parts * OUT_ROWS, B), BF),
        scratch_shapes=[
            pltpu.VMEM((parts * rows, own), BF),
            pltpu.VMEM((own // 256 * rows, 256), BF),
            pltpu.VMEM((parts, B, 8, B), F32),
        ],
        compiler_params=pltpu.CompilerParams(vmem_limit_bytes=32 << 20),
    )(me, query, mixed, taps, *grads)


def ungroup(me, x_ref, d_ref, m_ref, n_ref):
    shape = (16, 8, B)
    line = lax.broadcasted_iota(jnp.int32, shape, 1)
    lane = lax.broadcasted_iota(jnp.int32, shape, 2) // 32
    for half in range(2):
        lanes = pl.ds(B * half, B)
        for b in range(4):
            pairs = pl.ds(16 * b, 16)
            tiles = [x_ref[pairs, half, pl.ds(8 * u, 8)].astype(F32) for u in range(5)]
            chunks = [tiles[0]] + [
                jnp.roll(jnp.where(line < 2 * t, tiles[t + 1], tiles[t]), 8 - 2 * t, axis=1)
                for t in range(1, 4)
            ]
            taps = jnp.where((line == 6) | (line == 7), tiles[4], 0.0)
            for t in range(3):
                here = jnp.where((line == 2 * t) | (line == 2 * t + 1), tiles[t + 1], 0.0)
                taps = jnp.where(me == t, here, taps)
            taps = jnp.broadcast_to(0.5 * jnp.sum(taps, axis=1, keepdims=True), shape)
            n_ref[pairs, half] = taps
            turned = []
            for d in range(4):
                mix = chunks[(3 - d) % 4]
                for i in range(3):
                    mix = jnp.where(lane == i, chunks[(i - d) % 4], mix)
                turned.append(mix if d == 0 else jnp.roll(mix, B - 32 * d, axis=2))
            fours = []
            for i in range(4):
                mix = turned[(i - 3) % 4]
                for t in range(3):
                    mix = jnp.where(lane == t, turned[(i - t) % 4], mix)
                fours.append(mix)
            moved = [jnp.roll(x, 4, axis=1) for x in fours]
            top = line < 4
            delta = [jnp.where(top, fours[i], moved[i + 1]) for i in (0, 2)]
            mixed = [jnp.where(top, moved[i], fours[i + 1]) for i in (0, 2)]
            at = pl.ds(256 * b, 256)
            d_ref[at, lanes] = jnp.concatenate(delta, axis=1).reshape(256, B).astype(BF)
            m_ref[at, lanes] = jnp.concatenate(mixed, axis=1).reshape(256, B).astype(BF)


def regroup(part, sums, o_ref, tile, half):
    shape = (16, 8, B)
    row = lax.broadcasted_iota(jnp.int32, shape, 1)
    lane = lax.broadcasted_iota(jnp.int32, shape, 2) // 32
    low, high = part[:, :8], part[:, 8:]
    fours = [low, jnp.roll(low, 4, axis=1), high, jnp.roll(high, 4, axis=1)]
    turned = []
    for d in range(4):
        mix = fours[(3 + d) % 4]
        for t in range(3):
            mix = jnp.where(lane == t, fours[(t + d) % 4], mix)
        turned.append(mix if d == 0 else jnp.roll(mix, 32 * d, axis=2))
    coarse = sums.astype(BF).astype(F32)
    fine = sums - coarse
    coarse = jnp.broadcast_to(coarse[:, None], shape)
    fine = jnp.broadcast_to(fine[:, None], shape)
    rest = jnp.where(row == 4, coarse, jnp.where(row == 5, fine, 0.0))
    chunks = []
    for t in range(4):
        chunk = turned[(3 - t) % 4]
        for i in range(3):
            chunk = jnp.where(lane == i, turned[(i - t) % 4], chunk)
        chunk = jnp.where(row < 4, chunk, rest)
        chunks.append(chunk if t == 0 else jnp.roll(chunk, 8 - 2 * t, axis=1))
    for u in range(3):
        joined = jnp.where(row < 6 - 2 * u, chunks[u], chunks[u + 1])
        o_ref[pl.ds(16 * tile, 16), half, pl.ds(8 * u, 8)] = joined.astype(BF)


def correlate_kernel(
    me_ref, x_ref, o_ref, d_ref, m_ref, t_ref, f_ref, w_ref, qa_ref, qb_ref, l_ref, n_ref
):
    ungroup(me_ref[0], x_ref, d_ref, m_ref, n_ref)
    d_ref[pl.ds(1024, 256), :] = jnp.zeros((256, 256), BF)
    row = lax.broadcasted_iota(jnp.int32, (B, B), 0)
    col = lax.broadcasted_iota(jnp.int32, (B, B), 1)

    flip = jnp.where((row + col) % B == 0, 1.0, 0.0).astype(BF)
    taps = n_ref[...].reshape(1024, B).astype(BF)
    f_ref[...] = jnp.dot(taps, flip, preferred_element_type=F32).reshape(B, 8, B)
    lower = row >= col
    w_ref[pl.ds(0, B), pl.ds(B, B)] = jnp.zeros((B, B), BF)

    def build(e, before):
        line = jnp.broadcast_to(f_ref[pl.ds(e, 1)], (16, 8, B)).reshape(B, B)
        turned = pltpu.roll(line, 0, 1, stride=1, stride_axis=0)
        block = jnp.where(lower, turned, before).astype(BF)
        at = pl.multiple_of(e * B, B)
        w_ref[pl.ds(at, B), pl.ds(0, B)] = block
        w_ref[pl.ds(at + B, B), pl.ds(B, B)] = block
        return turned

    before = jnp.zeros((B, B), F32)
    mirror = jnp.where(row + col == B - 1, 1.0, 0.0).astype(BF)
    for half in range(2):
        t_ref[pl.ds(B * half, B), :] = lax.dot_general(
            mirror,
            m_ref[:, pl.ds(B * half, B)],
            (((1,), (1,)), ((), ())),
            preferred_element_type=F32,
        ).astype(BF)
    for part in range(4):
        depth = 256 * (4 - part)

        def gram(k, carry):
            e = 16 * part + k
            table = jnp.dot(
                t_ref[:, pl.ds(0, depth)],
                d_ref[pl.ds(pl.multiple_of(16 * e, 16), depth), :],
                preferred_element_type=F32,
            )
            qa_ref[2 * e] = table[:B, :B] + table[B:, B:]
            qa_ref[2 * e + 1] = table[:B, B:]
            qb_ref[e] = table[B:, :B]
            return build(2 * e + 1, build(2 * e, carry))

        before = lax.fori_loop(0, 16, gram, before, unroll=16)
    qb_ref[64] = jnp.zeros((B, B), F32)
    qa_ref[128] = jnp.zeros((B, B), F32)
    keep = row + col >= B - 1

    def diagonals(e, carry):
        first = qa_ref[2 * e]
        second = qa_ref[2 * e + 1] + qb_ref[e + 1]
        third = qa_ref[2 * e + 2]
        for u, (here, ahead) in enumerate(((first, second), (second, third))):
            turned = pltpu.roll(jnp.where(keep, here, ahead), 1, 1, stride=1, stride_axis=0)
            l_ref[pl.ds(2 * e + u, 1), :] = jnp.sum(turned, axis=0, keepdims=True)
        return carry

    for tile in range(4):
        count = 64 - 16 * tile
        left = jnp.concatenate(
            [d_ref[pl.ds(256 * tile + 16 * u, 256), :] for u in range(count)], axis=1
        )
        total = jnp.dot(left, w_ref[pl.ds(0, 256 * count), :], preferred_element_type=F32)
        for e in range(16 * tile, 16 * tile + 16):
            diagonals(e, 0)
        for half in range(2):
            part = total[:, B * half : B * half + B].reshape(16, GSIZE, B)
            sums = l_ref[pl.ds(32 * tile + half, 16, stride=2), :]
            regroup(part, sums, o_ref, tile, half)


def correlate(me, signals):
    return pl.pallas_call(
        correlate_kernel,
        in_specs=[
            pl.BlockSpec(memory_space=pltpu.SMEM),
            pl.BlockSpec(memory_space=pltpu.VMEM),
        ],
        out_specs=pl.BlockSpec(memory_space=pltpu.VMEM),
        out_shape=jax.ShapeDtypeStruct((64, 2, 4 * BACK_ROWS, B), BF),
        scratch_shapes=[
            pltpu.VMEM((1280, 256), BF),
            pltpu.VMEM((1024, 256), BF),
            pltpu.VMEM((256, 1024), BF),
            pltpu.VMEM((B, 8, B), F32),
            pltpu.VMEM((129 * B, 256), BF),
            pltpu.VMEM((129, B, B), F32),
            pltpu.VMEM((65, B, B), F32),
            pltpu.VMEM((B, B), F32),
            pltpu.VMEM((64, 2, 8, B), F32),
        ],
        compiler_params=pltpu.CompilerParams(vmem_limit_bytes=40 << 20),
        cost_estimate=pl.CostEstimate(
            flops=640 * 2 * 256**3, bytes_accessed=64 << 20, transcendentals=0
        ),
    )(me, signals)


def finish_kernel(me_ref, s_ref, q_ref, b_ref, o_ref, h_ref, l_ref, d_ref, sem):
    parts, rows, own = q_ref.shape
    steps = own // 256

    def send(source, plane, t):
        lanes = pl.ds(own * t, own)
        return pltpu.make_async_copy(source, o_ref.at[plane, :, lanes], sem.at[plane, t])

    copies = [send(q_ref.at[t], 0, t) for t in range(parts)]
    for copy in copies:
        copy.start()
    shape = (4 * B, 256)
    row = lax.broadcasted_iota(jnp.int32, shape, 0)
    col = lax.broadcasted_iota(jnp.int32, shape, 1)
    inner = row % B
    wanted = (inner // 8) * GSIZE + 4 * (row // B) + inner % 8
    spread = jnp.where((inner % 8 < 4) & (col == wanted), 1.0, 0.0).astype(BF)
    tiles = [b_ref[:, pl.ds(8 * u, 8)].astype(F32) for u in range(3)]
    line = lax.broadcasted_iota(jnp.int32, tiles[0].shape, 1)
    chunks = [tiles[0]]
    for t in range(1, parts):
        part = jnp.roll(tiles[t - 1], 2 * t, axis=1)
        if t < parts - 1:
            part = jnp.where(line < 2 * t, part, jnp.roll(tiles[t], 2 * t, axis=1))
        chunks.append(part)
    for t in range(parts):
        chunk = chunks[t].reshape(B * 8, B).astype(BF).T
        for i in range(4):
            for b in range(steps):
                l_ref[pl.ds((t * steps + b) * rows, rows), pl.ds(B * i, B)] = chunk[
                    rows * i : rows * i + rows, B * b : B * b + B
                ]
        span = steps * rows
        grad = jnp.dot(
            l_ref[pl.ds(t * span, span), :], spread, preferred_element_type=F32
        )
        for b in range(steps):
            lanes = pl.ds(own * t + 256 * b, 256)
            here = grad[b * rows : b * rows + rows]
            d_ref[0, :, lanes] = (here * s_ref[2, :, lanes].astype(F32)).astype(BF)
            d_ref[1, :, lanes] = (here * s_ref[1, :, lanes].astype(F32)).astype(BF)
        for plane in (1, 2):
            copy = send(d_ref.at[plane - 1, :, pl.ds(own * t, own)], plane, t)
            copy.start()
            copies.append(copy)
    tail = chunks[0]
    for t in range(1, parts):
        tail = jnp.where(me_ref[0] == t, chunks[t], tail)
    h_ref[...] = jnp.sum(jnp.where((line == 4) | (line == 5), tail, 0.0), axis=1).T
    for copy in copies:
        copy.wait()


def finish(me, saved, d_query, back):
    _, rows, width = saved.shape
    parts, _, own = d_query.shape
    vmem = pl.BlockSpec(memory_space=pltpu.VMEM)
    return pl.pallas_call(
        finish_kernel,
        in_specs=[pl.BlockSpec(memory_space=pltpu.SMEM), vmem, vmem, vmem],
        out_specs=[pl.BlockSpec(memory_space=pl.ANY), vmem],
        out_shape=(
            jax.ShapeDtypeStruct(saved.shape, BF),
            jax.ShapeDtypeStruct((B, own // GSIZE), F32),
        ),
        scratch_shapes=[
            pltpu.VMEM((parts * (own // 256) * rows, 4 * B), BF),
            pltpu.VMEM((2, rows, width), BF),
            pltpu.SemaphoreType.DMA((3, parts)),
        ],
        compiler_params=pltpu.CompilerParams(vmem_limit_bytes=32 << 20),
    )(me, saved, d_query, back)


def swap(x, axis):
    return lax.all_to_all(x, axis, split_axis=0, concat_axis=0, tiled=True)


def shift(chunks, axis):
    size = len(chunks)
    return [chunks[0]] + [
        lax.ppermute(chunks[k], axis, [(i, (i + k) % size) for i in range(size)])
        for k in range(1, size)
    ]


def per_device(saved_rows, grad_out, conv_out, filters):
    saved = saved_rows.transpose(1, 0, 2)
    _, rows, width = saved.shape
    tokens, own = grad_out.shape
    parts = width // own
    groups = own // GSIZE
    me = lax.axis_index("tp").reshape(1)
    own_rows = grad_out.reshape(parts, rows, own)
    grads = [
        lax.dynamic_index_in_dim(own_rows, lax.rem(me[0] + k, parts), 0, keepdims=False)
        for k in range(parts)
    ]
    *grads, after = lax.optimization_barrier((*grads, me))
    query, mixed, d_query, taps = prepare(after, saved, grad_out, conv_out, filters, parts)
    spread = pack(me, query, mixed, taps, shift(grads, "tp"))
    spread = spread.reshape(groups * parts, OUT_ROWS // 2, 2, tokens)
    signals, d_query = lax.optimization_barrier((swap(spread, ("ctx", "tp")), d_query))
    home_q = swap(d_query.reshape(parts, rows, own), "tp")
    answer = correlate(me, signals.reshape(groups // 2, 2, parts * OUT_ROWS, tokens))
    answer, home_q = lax.optimization_barrier((answer, home_q))
    back = swap(answer.reshape(groups * parts, BACK_ROWS // 2, 2, tokens), ("ctx", "tp"))
    back = back.reshape(groups, parts * BACK_ROWS, tokens)
    d_saved, d_filters = finish(me, saved, home_q, back)
    return (d_saved.transpose(1, 0, 2), d_filters)


def solution(mesh):
    placed = (P(("ctx", "tp"), None, None), P("ctx", "tp"), P("ctx", "tp"), P("ctx", "tp"))
    return jax.shard_map(
        per_device,
        mesh=mesh,
        in_specs=placed,
        out_specs=(P(("ctx", "tp"), None, None), P("ctx", "tp")),
        check_vma=False,
    )
```
